128 devices in a mesh: ax: 16 (over z, y), az: 8 (over x, core).
Axes of the slice: x: 4, y: 4, z: 4, core: 2. Of those that a mesh axis runs over, the one named last changes fastest.
Arguments:
- lamb_vector: bfloat16 [32768, 3, 512], P(('ax', 'az')), may hold values from -6 to 6
- owner: int32 [32768, 1], P(('ax', 'az')), may hold values from 0 to 127; in each aligned block of 256 rows (0 to 255, 256 to 511, ...) at most 6 rows name the same one
- element: int32 [32768], P(('ax', 'az')), may hold values from 0 to 1023
- shape_class: int32 [32768], P(('ax', 'az')), may hold values from 0 to 1
- interp_tables: bfloat16 [2, 512, 125], replicated, may hold values from -0.25 to 0.25
- acoustic_state: float32 [5, 125, 32, 32, 128], P(None, None, 'ax', 'az'), may hold values from -6 to 6
Outputs:
- new_state: float32 [5, 125, 32, 32, 128], P(None, None, 'ax', 'az')
- source: float32 [3, 125, 32, 32, 128], P(None, None, 'ax', 'az')
The draws below stay inside these ranges and needn't reach their ends.
Inputs may be any that keep to these rules, and one draw needn't show every extreme that they name: `owner`: among one device's 256 flow elements no device is named by more than 6 of them, and some device is named by exactly 6.
All inputs are finite; a program needn't handle non-finite values.
Results may differ from the reference program's by a relative error of at most 0.0013.
Values may be sent and summed in bfloat16 or wider, within the bound.
A program may use at most 128 MiB of HBM per device.

```python
import math
import jax
import jax.numpy as jnp
import numpy as np
from jax import lax

NF = 512
NA = 125
FIELDS = 5
NTAB = 2
FE_DEV = 256
EX = 2
EY = 4
ER = 128
CAP = 6
AE_DEV = 1024
FLOW = 32768
NXE = 32
NYE = 32
N_AX = 16
N_AZ = 8
DEVICES = 128


def touch_ends(entries, key, smallest, largest):
    longest = entries.shape.index(max(entries.shape))
    spots = []
    for shift in (0, 1):
        where = [jax.random.randint(jax.random.fold_in(key, axis), (), 0, length) for axis, length in enumerate(entries.shape)]
        where[longest] = (where[longest] + shift) % entries.shape[longest]
        spots.append(tuple(where))
    return entries.at[spots[0]].set(smallest).at[spots[1]].set(largest)


def shard_levels(stream_key, extent, split, low, largest):
    gain, own = 1.0, jax.random.fold_in(stream_key, 6)
    for axis_at, shards_of in split:
        steps = jnp.exp(jax.random.uniform(jax.random.fold_in(own, axis_at), (shards_of,), jnp.float32, low / len(split), largest / len(split)))
        gain = gain * jnp.repeat(steps, extent[axis_at] // shards_of).reshape([-1 if axis == axis_at else 1 for axis in range(len(extent))])
    return gain


def routed_block(rng, own, number, rows, count, top, bound, skew):
    order = jax.random.permutation(rng, count)
    packed, common = shares(count, rows * top, bound, skew, True), shares(count, rows * top, bound, skew, False)
    places = jnp.arange(count)

    def named(sizes, rotation):
        used = int((sizes > 0).sum())
        fixed = max(1, used // 4)
        shifted = fixed + (places - fixed + rotation * (used - fixed)) % max(1, count - fixed)
        return jnp.zeros((count,), jnp.int32).at[order[jnp.where(places < fixed, places, shifted)]].set(jnp.asarray(sizes, jnp.int32))

    sizes = jnp.where(number % 4 == 0, named(packed, number // 4), named(common, number - number // 4 - 1))
    mixed = jax.random.permutation(jax.random.fold_in(own, 3), count)
    donor, taker = mixed[0:count // 2 * 2:2], mixed[1:count // 2 * 2:2]
    slack = jnp.minimum(sizes[donor] - 1, bound - sizes[taker]) // 2
    slack = jnp.where((donor == order[0]) | (taker == order[0]) | (sizes[taker] == 0), 0, jnp.maximum(slack, 0))
    shifted = jax.random.randint(jax.random.fold_in(own, 4), (count // 2,), 0, 1 << 20) % (slack + 1)
    sizes = sizes.at[donor].add(-shifted).at[taker].add(shifted)
    labels = jnp.searchsorted(jnp.cumsum(sizes), jnp.arange(rows * top), side="right").astype(jnp.int32)
    grid = labels.reshape(top, rows).T
    grid = grid[jax.random.permutation(jax.random.fold_in(own, 1), rows)]
    rotation = jax.random.randint(jax.random.fold_in(own, 2), (rows, 1), 0, top)
    return jnp.take_along_axis(grid, (jnp.arange(top)[None, :] + rotation) % top, axis=1)


def shares(number_of, total, reach, skew, full):
    portions = [(1 << 20) // math.isqrt(rank ** skew) + 1 for rank in range(1, number_of + 1)]
    largest = reach if full else min(reach, max(-(-total // number_of), total * portions[0] // sum(portions)))
    least = 1 if total - largest >= number_of - 1 else 0
    holding, spare = [largest] + [least] * (number_of - 1), total - largest - least * (number_of - 1)
    while spare > 0:
        free = [i for i in range(1, number_of) if holding[i] < largest] or [i for i in range(1, number_of) if holding[i] < reach]
        mass, budget = sum([portions[i] for i in free]), spare
        for i in free:
            more = min(reach - holding[i], max(1, budget * portions[i] // mass), spare)
            holding[i] = holding[i] + more
            spare = spare - more
    return np.array(holding)


def bell_draw(own_key, extent, deviation, limit, cuts=(), kind=jnp.bfloat16):
    values = jax.random.normal(own_key, extent, jnp.float32) * deviation
    if len(cuts) > 0:
        values = shard_levels(own_key, extent, cuts, -0.22, 0.18) * values
    return jnp.clip(values, min=-limit, max=limit).astype(kind)


def setup_inputs(seed: int = 0) -> dict:
    splits = jax.random.split(jax.random.key(seed), 7)
    lamb_vector = bell_draw(splits[0], (FLOW, 3, NF), 1.0, 6.0, ((0, 128),))
    owner_keys = jax.random.split(jax.random.fold_in(splits[1], 1), FLOW // FE_DEV)
    owner_turns = jax.random.permutation(jax.random.fold_in(splits[1], 3), FLOW // FE_DEV)
    owner = jax.vmap(lambda own, number: routed_block(jax.random.fold_in(splits[1], 2), own, number, FE_DEV, DEVICES, 1, CAP, 2))(owner_keys, owner_turns).reshape((FLOW, 1))
    element = touch_ends(jax.random.randint(splits[2], (FLOW,), 0, AE_DEV), jax.random.fold_in(splits[2], 1), 0, AE_DEV - 1).astype(jnp.int32)
    shape_class = touch_ends(jax.random.randint(splits[3], (FLOW,), 0, NTAB), jax.random.fold_in(splits[3], 1), 0, NTAB - 1).astype(jnp.int32)
    interp_tables = bell_draw(splits[4], (NTAB, NF, NA), NF ** -0.5, 0.25)
    acoustic_state = bell_draw(splits[5], (FIELDS, NA, NXE, NYE, ER), 1.0, 6.0, ((2, 16), (3, 8)), jnp.float32)
    return {"lamb_vector": lamb_vector, "owner": owner, "element": element, "shape_class": shape_class, "interp_tables": interp_tables, "acoustic_state": acoustic_state}


MACH_NUMBER = 0.3
RUSANOV_SPEED = 1.3
TIME_STEP = 0.03
LIFT_FACTOR = 10.0
VOLUME_FACTOR = 2.0

def gll_tables():
    points = np.array([-1.0, -math.sqrt(3.0 / 7.0), 0.0, math.sqrt(3.0 / 7.0), 1.0])
    barycentric = np.array([1.0 / np.prod([points[col_index] - points[other_index] for other_index in range(5) if other_index != col_index]) for col_index in range(5)])
    derivative = np.zeros((5, 5))
    for row_index in range(5):
        for col_index in range(5):
            if row_index != col_index:
                derivative[row_index, col_index] = barycentric[col_index] / barycentric[row_index] / (points[row_index] - points[col_index])
        derivative[row_index, row_index] = -np.sum(derivative[row_index])
    identity = np.eye(5)
    return [np.kron(np.kron(derivative, identity), identity), np.kron(np.kron(identity, derivative), identity), np.kron(np.kron(identity, identity), derivative)]

def flux(field, direction):
    pressure = field[0]
    axial = field[1]
    azimuthal = field[2]
    radial = field[3]
    density = field[4]
    nothing = jnp.zeros_like(pressure)
    gradient = MACH_NUMBER * axial + pressure
    if direction == 0:
        return jnp.stack([MACH_NUMBER * pressure + axial, gradient, nothing, nothing, MACH_NUMBER * density + axial])
    if direction == 1:
        return jnp.stack([azimuthal, nothing, gradient, nothing, azimuthal])
    return jnp.stack([radial, nothing, nothing, gradient, radial])

def face_term(inner, outer, direction, normal):
    jump = inner - outer
    return LIFT_FACTOR * (normal * flux(jump, direction) - RUSANOV_SPEED * jump)

def node_faces(state):
    trailing = state.shape[2:]
    count = state.shape[0]
    shaped = state.reshape((count, 5, 5, 5) + trailing)
    result = []
    for picked in [shaped[:, 0], shaped[:, 4], shaped[:, :, 0], shaped[:, :, 4], shaped[:, :, :, 0], shaped[:, :, :, 4]]:
        result.append(picked.reshape((count, 25) + trailing))
    return result

def add_faces(total, terms):
    trailing = total.shape[2:]
    count = total.shape[0]
    shaped = total.reshape((count, 5, 5, 5) + trailing)
    pieces = [term.reshape((count, 5, 5) + trailing) for term in terms]
    shaped = shaped.at[:, 0].add(pieces[0])
    shaped = shaped.at[:, 4].add(pieces[1])
    shaped = shaped.at[:, :, 0].add(pieces[2])
    shaped = shaped.at[:, :, 4].add(pieces[3])
    shaped = shaped.at[:, :, :, 0].add(pieces[4])
    shaped = shaped.at[:, :, :, 4].add(pieces[5])
    return shaped.reshape(total.shape)

def volume(state):
    tables = gll_tables()
    total = jnp.zeros_like(state)
    for direction in range(3):
        matrix = jnp.asarray(tables[direction], jnp.float32)
        gradient = jnp.einsum('ij,fjxyz->fixyz', matrix, state, precision=lax.Precision.HIGHEST)
        total = total - VOLUME_FACTOR * flux(gradient, direction)
    return total

def radial_outer(minus_face, plus_face):
    widths_low = ((0, 0), (0, 0), (0, 0), (0, 0), (1, 0))
    widths_high = ((0, 0), (0, 0), (0, 0), (0, 0), (0, 1))
    return (jnp.pad(plus_face, widths_low)[..., :-1], jnp.pad(minus_face, widths_high)[..., 1:])

def operate(state, source):
    faces = node_faces(state)
    outer_xm = jnp.pad(faces[1], ((0, 0), (0, 0), (1, 0), (0, 0), (0, 0)))[:, :, :-1]
    outer_xp = jnp.pad(faces[0], ((0, 0), (0, 0), (0, 1), (0, 0), (0, 0)))[:, :, 1:]
    outer_ym = jnp.roll(faces[3], 1, axis=3)
    outer_yp = jnp.roll(faces[2], -1, axis=3)
    outer_zm, outer_zp = radial_outer(faces[4], faces[5])
    terms = [face_term(faces[0], outer_xm, 0, -1.0), face_term(faces[1], outer_xp, 0, 1.0), face_term(faces[2], outer_ym, 1, -1.0), face_term(faces[3], outer_yp, 1, 1.0), face_term(faces[4], outer_zm, 2, -1.0), face_term(faces[5], outer_zp, 2, 1.0)]
    total = add_faces(volume(state), terms)
    return total.at[1:4].add(source)

def reference(lamb_vector, owner, element, shape_class, interp_tables, acoustic_state):
    devices = N_AX * N_AZ
    global_elements = NXE * NYE * ER
    target = owner[:, 0]
    axial_index = target // N_AZ
    azimuth_index = target % N_AZ
    elem_axial = element // (EY * ER)
    elem_azimuth = element // ER % EY
    elem_radial = element % ER
    global_index = ((axial_index * EX + elem_axial) * NYE + azimuth_index * EY + elem_azimuth) * ER + elem_radial
    keys = (shape_class * global_elements + global_index).astype(jnp.int32)
    blocks = lamb_vector.reshape(devices, FE_DEV, 3 * NF)
    key_blocks = keys.reshape(devices, FE_DEV)

    def accumulate(carry, pair):
        block, block_keys = pair
        return (carry.at[block_keys].add(block.astype(jnp.float32)), None)
    gathered, _ = lax.scan(accumulate, jnp.zeros((NTAB * global_elements, 3 * NF), jnp.float32), (blocks, key_blocks))
    gathered = gathered.reshape(NTAB, global_elements, 3, NF)
    source = jnp.einsum('keci,kij->cje', gathered, interp_tables.astype(jnp.float32), precision=lax.Precision.HIGHEST)
    source = source.reshape(3, NA, NXE, NYE, ER)
    first = operate(acoustic_state, source)
    second = operate(acoustic_state + 0.5 * TIME_STEP * first, source)
    third = operate(acoustic_state + 0.5 * TIME_STEP * second, source)
    fourth = operate(acoustic_state + TIME_STEP * third, source)
    new_state = acoustic_state + TIME_STEP / 6.0 * (first + 2.0 * second + 2.0 * third + fourth)
    return (new_state, source)
```

```python
import functools
import math

import jax
import jax.numpy as jnp
import numpy as np
from jax import lax
from jax.experimental import pallas as pl
from jax.experimental.pallas import tpu as pltpu
from jax.sharding import PartitionSpec as P

MACH = 0.3
SPEED = 1.3
DT = 0.03
LIFT = 10.0
VOLUME = 2.0
SLOTS = 6
MESH = pl.DeviceIdType.MESH
F32 = jnp.float32
BF16 = jnp.bfloat16


def line_matrix():
    points = [-1.0, -math.sqrt(3.0 / 7.0), 0.0, math.sqrt(3.0 / 7.0), 1.0]
    bary = [
        1.0 / math.prod(points[c] - points[o] for o in range(5) if o != c) for c in range(5)
    ]
    d = np.zeros((5, 5))
    for i in range(5):
        for j in range(5):
            if i != j:
                d[i, j] = bary[j] / bary[i] / (points[i] - points[j])
        d[i, i] = -np.sum(d[i])
    return -VOLUME * d


D = line_matrix()


def deriv(x):
    e0, e1, o0, o1 = x[0] + x[4], x[1] + x[3], x[0] - x[4], x[1] - x[3]
    y = [None] * 5
    for i in range(2):
        odd = float(0.5 * (D[i, 0] - D[i, 4])) * o0 + float(0.5 * (D[i, 1] - D[i, 3])) * o1
        even = (
            float(0.5 * (D[i, 0] + D[i, 4])) * e0
            + float(0.5 * (D[i, 1] + D[i, 3])) * e1
            + float(D[i, 2]) * x[2]
        )
        y[i], y[4 - i] = odd + even, odd - even
    y[2] = float(D[2, 0]) * o0 + float(D[2, 1]) * o1
    return y


def cross_terms(jump, normal, along):
    t = (LIFT * normal) * jump[along]
    out = [None] * 5
    for f in (0, 4):
        out[f] = t - (LIFT * SPEED) * jump[f]
    for f in (1, 2, 3):
        out[f] = (-LIFT * SPEED) * jump[f]
    g = MACH * jump[1] + jump[0]
    out[along] = out[along] + (LIFT * normal) * g
    return out


def axial_terms(jump, normal):
    p, u, v, w, d = jump
    near = LIFT * (normal * MACH - SPEED)
    t = (LIFT * normal) * u
    return [
        near * p + t,
        near * u + (LIFT * normal) * p,
        (-LIFT * SPEED) * v,
        (-LIFT * SPEED) * w,
        near * d + t,
    ]


def kernel(
    nax, naz,
    state_hbm, lamb_ref, table_ref, owner_ref, element_ref, class_ref,
    new_hbm, source_hbm,
    q_ref, bufs, acc, s_ref, post, inbox,
    xs, xl, xr, ys, yl, yr,
    state_sem, self_sem, mail_send, mail_recv, xsend, xrecv, ysend, yrecv, out_sem,
):
    n = nax * naz
    ax, az = lax.axis_index("ax"), lax.axis_index("az")
    me = ax * naz + az
    has_left, has_right = ax > 0, ax < nax - 1
    az_up, az_down = lax.rem(az + 1, naz), lax.rem(az + naz - 1, naz)
    row = lax.broadcasted_iota(jnp.int32, (8, 128), 0)
    lane = lax.broadcasted_iota(jnp.int32, (8, 128), 1)
    low_half = row < 4
    ey = row & 3

    load_state = pltpu.make_async_copy(state_hbm, q_ref, state_sem)
    load_state.start()

    def clear(i, carry):
        inbox[i] = jnp.zeros(inbox.shape[1:], F32)
        return carry

    lax.fori_loop(0, n, clear, 0)

    @pl.when(jnp.logical_not(has_left))
    def _():
        def body(i, carry):
            for k in range(4):
                xl[k, i] = jnp.zeros(xl.shape[2:], BF16)
            return carry
        lax.fori_loop(0, 5, body, 0)

    @pl.when(jnp.logical_not(has_right))
    def _():
        def body(i, carry):
            for k in range(4):
                xr[k, i] = jnp.zeros(xr.shape[2:], BF16)
            return carry
        lax.fori_loop(0, 5, body, 0)

    barrier = pltpu.get_barrier_semaphore()

    def greet(i, carry):
        other = lax.rem(me + i, n)
        pl.semaphore_signal(
            barrier, inc=1, device_id=(other // naz, lax.rem(other, naz)), device_id_type=MESH
        )
        return carry

    lax.fori_loop(1, n, greet, 0)

    owner, element, shape_class = owner_ref[...], element_ref[...], class_ref[...]
    count = owner.shape[1]
    hit = lax.broadcasted_iota(jnp.int32, (n, count), 0) == owner
    hit = jnp.where(hit, 1.0, 0.0)
    earlier = lax.broadcasted_iota(jnp.int32, (count, count), 0) < lax.broadcasted_iota(
        jnp.int32, (count, count), 1
    )
    ranks = jnp.dot(
        hit.astype(BF16), jnp.where(earlier, 1.0, 0.0).astype(BF16), preferred_element_type=F32
    )
    position = jnp.sum(hit * ranks, axis=0, keepdims=True).astype(jnp.int32)
    slot = owner * 8 + position
    place = lax.broadcasted_iota(jnp.int32, (n * 8, count), 0) == slot
    place = jnp.where(place, 1.0, 0.0).astype(BF16)
    node_row = lax.broadcasted_iota(jnp.int32, (128, count), 0)
    for c in range(3):
        both = lax.dot_general(
            table_ref[...], lamb_ref[c], (((1,), (1,)), ((), ())), preferred_element_type=F32
        )
        value = jnp.where(shape_class == 0, both[:128], both[128:])
        if c == 0:
            value = jnp.where(node_row == 125, ((element >> 5) + 1).astype(F32), value)
            value = jnp.where(node_row == 126, (element & 31).astype(F32), value)
        high = value.astype(BF16)
        low = (value - high.astype(F32)).astype(BF16)
        mail = lax.dot_general(
            place, jnp.concatenate([high, low], axis=0), (((1,), (1,)), ((), ())),
            preferred_element_type=F32,
        )
        post[:, c] = (mail[:, :128] + mail[:, 128:]).reshape(n, 8, 128)

    def x_copy(k, b, side):
        if side == 0:
            dst, dev = xl, (ax + 1, az)
        else:
            dst, dev = xr, (ax - 1, az)
        return pltpu.make_async_remote_copy(
            src_ref=xs.at[k, b, side], dst_ref=dst.at[k, b], send_sem=xsend.at[k, b, side],
            recv_sem=xrecv.at[k, b, side], device_id=dev, device_id_type=MESH,
        )

    def y_copy(k, side):
        if side == 0:
            dst, dev = yl, (ax, az_up)
        else:
            dst, dev = yr, (ax, az_down)
        return pltpu.make_async_remote_copy(
            src_ref=ys.at[k, side], dst_ref=dst.at[k], send_sem=ysend.at[k, side],
            recv_sem=yrecv.at[k, side], device_id=dev, device_id_type=MESH,
        )

    def pack_x(ref, k, b):
        for side in range(2):
            a = 4 if side == 0 else 0
            parts = []
            for m in range(14):
                pair = []
                for q in (2 * m, 2 * m + 1):
                    pair.append(ref[q % 5, a, b, q // 5] if q < 25 else jnp.zeros((8, 128), F32))
                even, odd = pltpu.roll(pair[0], 4, 0), pair[1]
                parts.append(
                    jnp.where(low_half, even, odd) if side == 0 else jnp.where(low_half, odd, even)
                )
            for t in range(7):
                xs[k, b, side, 16 * t:16 * t + 16, :] = jnp.concatenate(
                    [parts[2 * t], parts[2 * t + 1]], axis=0
                ).astype(BF16)

    def pack_y(ref, k, side):
        b = 4 if side == 0 else 0

        def body(a, carry):
            parts = []
            for m in range(8):
                total = jnp.zeros((8, 128), F32)
                for j in range(4):
                    q = 4 * m + j
                    if q < 25:
                        turn = (j - 3) % 8 if side == 0 else (3 + j) % 8
                        value = ref[q % 5, a, b, q // 5]
                        value = pltpu.roll(value, turn, 0) if turn else value
                        residue = j if side == 0 else (3 + j) % 4
                        total = jnp.where(ey == residue, value, total)
                parts.append(total)
            for t in range(4):
                ys[k, side, a, 16 * t:16 * t + 16, :] = jnp.concatenate(
                    [parts[2 * t], parts[2 * t + 1]], axis=0
                ).astype(BF16)
            return carry

        lax.fori_loop(0, 5, body, 0)

    def send_x(k, b):
        @pl.when(has_right)
        def _():
            x_copy(k, b, 0).start()

        @pl.when(has_left)
        def _():
            x_copy(k, b, 1).start()

    load_state.wait()

    def first_x(b, carry):
        pack_x(q_ref, 0, b)
        return carry

    lax.fori_loop(0, 5, first_x, 0)
    pack_y(q_ref, 0, 0)
    pack_y(q_ref, 0, 1)

    pl.semaphore_wait(barrier, n - 1)

    y_copy(0, 0).start()
    y_copy(0, 1).start()

    def first_send(b, carry):
        send_x(0, b)
        return carry

    lax.fori_loop(0, 5, first_send, 0)

    def mail_copy(other):
        return pltpu.make_async_remote_copy(
            src_ref=post.at[other, :, pl.ds(0, SLOTS)], dst_ref=inbox.at[me, :, pl.ds(0, SLOTS)],
            send_sem=mail_send, recv_sem=mail_recv,
            device_id=(other // naz, lax.rem(other, naz)), device_id_type=MESH,
        )

    def mail_out(i, carry):
        mail_copy(lax.rem(me + i, n)).start()
        return carry

    lax.fori_loop(1, n, mail_out, 0)
    inbox[me] = post[me]

    def z_pass(cur, nxt):
        def body(a, carry):
            for b in range(5):
                x = [[cur[f, a, b, r] for r in range(5)] for f in range(5)]
                dw = deriv(x[3])
                dg = deriv([MACH * x[1][r] + x[0][r] for r in range(5)])
                lo = cross_terms(
                    [x[f][0] - jnp.where(lane == 0, 0.0, pltpu.roll(x[f][4], 1, 1)) for f in range(5)],
                    -1.0, 3,
                )
                hi = cross_terms(
                    [x[f][4] - jnp.where(lane == 127, 0.0, pltpu.roll(x[f][0], 127, 1)) for f in range(5)],
                    1.0, 3,
                )
                for r in range(5):
                    for f in range(5):
                        value = dw[r] if f in (0, 4) else dg[r] if f == 3 else None
                        face = lo[f] if r == 0 else hi[f] if r == 4 else None
                        if value is None:
                            value = jnp.zeros((8, 128), F32) if face is None else face
                        elif face is not None:
                            value = value + face
                        nxt[f, a, b, r] = value
            return carry

        lax.fori_loop(0, 5, body, 0)

    def y_pass(cur, nxt, k):
        y_copy(k, 0).wait_recv()
        y_copy(k, 1).wait_recv()

        def body(a, carry):
            down, up = [], []
            for t in range(4):
                wide = yl[k, a, 16 * t:16 * t + 16, :].astype(F32)
                down += [wide[:8], wide[8:]]
                wide = yr[k, a, 16 * t:16 * t + 16, :].astype(F32)
                up += [wide[:8], wide[8:]]
            for r in range(5):
                x = [[cur[f, a, b, r] for b in range(5)] for f in range(5)]
                dv = deriv(x[2])
                dg = deriv([MACH * x[1][b] + x[0][b] for b in range(5)])
                jump_lo, jump_hi = [], []
                for f in range(5):
                    q = 5 * r + f
                    j = q % 4
                    halo = jnp.where(ey == j, down[q // 4], up[q // 4])
                    halo = pltpu.roll(halo, 8 - j, 0) if j else halo
                    jump_lo.append(x[f][0] - jnp.where(ey == 0, halo, pltpu.roll(x[f][4], 1, 0)))
                    jump_hi.append(x[f][4] - jnp.where(ey == 3, halo, pltpu.roll(x[f][0], 7, 0)))
                lo, hi = cross_terms(jump_lo, -1.0, 2), cross_terms(jump_hi, 1.0, 2)
                for b in range(5):
                    for f in range(5):
                        value = dv[b] if f in (0, 4) else dg[b] if f == 2 else None
                        face = lo[f] if b == 0 else hi[f] if b == 4 else None
                        if value is None and face is None:
                            continue
                        if value is None:
                            value = face
                        elif face is not None:
                            value = value + face
                        nxt[f, a, b, r] = nxt[f, a, b, r] + value
            return carry

        lax.fori_loop(0, 5, body, 0)

    def x_pass(cur, nxt, k, scale, first):
        def body(i, carry):
            b = jnp.where(i == 0, 0, jnp.where(i == 1, 4, i - 1))

            @pl.when(has_left)
            def _():
                x_copy(k, b, 0).wait_recv()

            @pl.when(has_right)
            def _():
                x_copy(k, b, 1).wait_recv()

            left, right = [], []
            for t in range(7):
                wide = xl[k, b, 16 * t:16 * t + 16, :].astype(F32)
                left += [wide[:8], wide[8:]]
                wide = xr[k, b, 16 * t:16 * t + 16, :].astype(F32)
                right += [wide[:8], wide[8:]]
            for r in range(5):
                x = [[cur[f, a, b, r] for a in range(5)] for f in range(5)]
                p, u, d = x[0], x[1], x[4]
                diff = {
                    0: deriv([MACH * p[a] + u[a] for a in range(5)]),
                    1: deriv([MACH * u[a] + p[a] for a in range(5)]),
                    4: deriv([MACH * d[a] + u[a] for a in range(5)]),
                }
                jump_lo, jump_hi = [], []
                for f in range(5):
                    q = 5 * r + f
                    m = q // 2
                    if q % 2 == 0:
                        halo = jnp.where(low_half, left[m], right[m])
                    else:
                        halo = pltpu.roll(jnp.where(low_half, right[m], left[m]), 4, 0)
                    own = pltpu.roll(jnp.where(low_half, x[f][4], x[f][0]), 4, 0)
                    jump_lo.append(x[f][0] - jnp.where(low_half, halo, own))
                    jump_hi.append(x[f][4] - jnp.where(low_half, own, halo))
                lo, hi = axial_terms(jump_lo, -1.0), axial_terms(jump_hi, 1.0)
                for a in range(5):
                    for f in range(5):
                        total = nxt[f, a, b, r]
                        if f in diff:
                            total = total + diff[f][a]
                        if a in (0, 4):
                            total = total + (lo[f] if a == 0 else hi[f])
                        if first and f in (1, 2, 3):
                            at = ((f - 1) * 125 + a * 25 + b * 5 + r) * 8
                            total = total + s_ref[pl.ds(pl.multiple_of(at, 8), 8), :]
                        total = scale * total
                        nxt[f, a, b, r] = total
                        before = q_ref[f, a, b, r] if first else acc[f, a, b, r]
                        acc[f, a, b, r] = before + total

            def hand_on():
                pack_x(nxt, k + 1, b)
                send_x(k + 1, b)

                @pl.when(i == 0)
                def _():
                    pack_y(nxt, k + 1, 1)
                    y_copy(k + 1, 1).start()

                @pl.when(i == 1)
                def _():
                    pack_y(nxt, k + 1, 0)
                    y_copy(k + 1, 0).start()

            if first:
                hand_on()
            else:
                pl.when(k < 3)(hand_on)
            return carry

        lax.fori_loop(0, 5, body, 0)

    z_pass(q_ref, bufs.at[0])
    y_pass(q_ref, bufs.at[0], 0)

    arrived = pltpu.make_async_remote_copy(
        src_ref=post.at[pl.ds(0, n - 1), :, pl.ds(0, SLOTS)],
        dst_ref=inbox.at[pl.ds(0, n - 1), :, pl.ds(0, SLOTS)],
        send_sem=mail_send, recv_sem=mail_recv,
        device_id=(ax, az), device_id_type=MESH,
    )
    arrived.wait_recv()
    turned = []
    code = None
    for c in range(3):
        block = inbox[:, c].reshape(n * 8, 128)
        if c == 0:
            code = ((block[:, 125:126] - 1.0) * 32.0 + block[:, 126:127]).astype(jnp.int32)
        turned.append(block.T)
    turned = jnp.concatenate(turned, axis=0)
    high = turned.astype(BF16)
    low = (turned - high.astype(F32)).astype(BF16)

    def spread(t, carry):
        member = code == lax.broadcasted_iota(jnp.int32, (n * 8, 256), 1) + 256 * t
        member = jnp.where(member, 1.0, 0.0).astype(BF16)
        total = jnp.dot(high, member, preferred_element_type=F32)
        total = total + jnp.dot(low, member, preferred_element_type=F32)
        for c in range(3):
            for h in range(2):
                s_ref[pl.ds(c * 1000 + 2 * t + h, 125, stride=8), :] = total[
                    128 * c:128 * c + 125, 128 * h:128 * h + 128
                ]
        return carry

    lax.fori_loop(0, 4, spread, 0)
    save_source = pltpu.make_async_copy(s_ref, source_hbm, out_sem.at[0])
    save_source.start()

    x_pass(q_ref, bufs.at[0], 0, DT, True)

    def stage(k, carry):
        cur, nxt = bufs.at[lax.rem(k + 1, 2)], bufs.at[lax.rem(k, 2)]
        scale = jnp.where(k == 1, DT / 2.0, jnp.where(k == 2, DT / 3.0, DT / 4.0))
        z_pass(cur, nxt)
        y_pass(cur, nxt, k)
        x_pass(cur, nxt, k, scale, False)
        return carry

    lax.fori_loop(1, 4, stage, 0)
    save_new = pltpu.make_async_copy(acc, new_hbm, out_sem.at[1])
    save_new.start()

    arrived.wait_send()

    def drain(k, carry):
        y_copy(k, 0).wait_send()
        y_copy(k, 1).wait_send()

        def inner(b, carry):
            @pl.when(has_right)
            def _():
                x_copy(k, b, 0).wait_send()

            @pl.when(has_left)
            def _():
                x_copy(k, b, 1).wait_send()
            return carry

        lax.fori_loop(0, 5, inner, 0)
        return carry

    lax.fori_loop(0, 4, drain, 0)
    save_source.wait()
    save_new.wait()


def body(nax, naz, lamb_vector, owner, element, shape_class, interp_tables, acoustic_state):
    n = nax * naz
    count = lamb_vector.shape[0]
    lamb = jnp.transpose(lamb_vector, (1, 0, 2))
    table = jnp.pad(jnp.transpose(interp_tables, (0, 2, 1)), ((0, 0), (0, 3), (0, 0)))
    table = table.reshape(256, 512)
    state = acoustic_state.reshape(5, 5, 5, 5, 8, 128)
    vmem, anywhere = pl.BlockSpec(memory_space=pltpu.VMEM), pl.BlockSpec(memory_space=pl.ANY)
    dma = pltpu.SemaphoreType.DMA
    new, source = pl.pallas_call(
        functools.partial(kernel, nax, naz),
        out_shape=(
            jax.ShapeDtypeStruct((5, 5, 5, 5, 8, 128), F32),
            jax.ShapeDtypeStruct((3000, 128), F32),
        ),
        in_specs=[anywhere, vmem, vmem, vmem, vmem, vmem],
        out_specs=(anywhere, anywhere),
        scratch_shapes=[
            pltpu.VMEM((5, 5, 5, 5, 8, 128), F32),
            pltpu.VMEM((2, 5, 5, 5, 5, 8, 128), F32),
            pltpu.VMEM((5, 5, 5, 5, 8, 128), F32),
            pltpu.VMEM((3000, 128), F32),
            pltpu.VMEM((n, 3, 8, 128), F32),
            pltpu.VMEM((n, 3, 8, 128), F32),
            pltpu.VMEM((4, 5, 2, 112, 128), BF16),
            pltpu.VMEM((4, 5, 112, 128), BF16),
            pltpu.VMEM((4, 5, 112, 128), BF16),
            pltpu.VMEM((4, 2, 5, 64, 128), BF16),
            pltpu.VMEM((4, 5, 64, 128), BF16),
            pltpu.VMEM((4, 5, 64, 128), BF16),
            dma, dma, dma, dma,
            dma((4, 5, 2)), dma((4, 5, 2)), dma((4, 2)), dma((4, 2)), dma((2,)),
        ],
        compiler_params=pltpu.CompilerParams(
            collective_id=0, has_side_effects=True, vmem_limit_bytes=50 * 1024 * 1024
        ),
    )(
        state, lamb, table,
        owner.reshape(1, count), element.reshape(1, count), shape_class.reshape(1, count),
    )
    return new.reshape(5, 125, 2, 4, 128), source.reshape(3, 125, 2, 4, 128)


def solution(mesh):
    nax, naz = mesh.shape["ax"], mesh.shape["az"]
    in_specs = (
        P(("ax", "az"), None, None),
        P(("ax", "az"), None),
        P(("ax", "az")),
        P(("ax", "az")),
        P(),
        P(None, None, "ax", "az", None),
    )
    out_specs = (P(None, None, "ax", "az", None), P(None, None, "ax", "az", None))
    return jax.shard_map(
        functools.partial(body, nax, naz), mesh=mesh, in_specs=in_specs, out_specs=out_specs,
        check_vma=False,
    )
```

```python
import functools
import math

import jax
import jax.numpy as jnp
import numpy as np
from jax import lax
from jax.experimental import pallas as pl
from jax.experimental.pallas import tpu as pltpu
from jax.sharding import PartitionSpec as P

MACH = 0.3
SPEED = 1.3
DT = 0.03
LIFT = 10.0
VOLUME = 2.0
MAIL = 9
GROUP = 16
MESH = pl.DeviceIdType.MESH
F32 = jnp.float32
BF16 = jnp.bfloat16


def line_matrix():
    points = [-1.0, -math.sqrt(3.0 / 7.0), 0.0, math.sqrt(3.0 / 7.0), 1.0]
    bary = [
        1.0 / math.prod(points[c] - points[o] for o in range(5) if o != c) for c in range(5)
    ]
    d = np.zeros((5, 5))
    for i in range(5):
        for j in range(5):
            if i != j:
                d[i, j] = bary[j] / bary[i] / (points[i] - points[j])
        d[i, i] = -np.sum(d[i])
    return -VOLUME * d


D = line_matrix()


def deriv(x):
    e0, e1, o0, o1 = x[0] + x[4], x[1] + x[3], x[0] - x[4], x[1] - x[3]
    y = [None] * 5
    for i in range(2):
        odd = float(0.5 * (D[i, 0] - D[i, 4])) * o0 + float(0.5 * (D[i, 1] - D[i, 3])) * o1
        even = (
            float(0.5 * (D[i, 0] + D[i, 4])) * e0
            + float(0.5 * (D[i, 1] + D[i, 3])) * e1
            + float(D[i, 2]) * x[2]
        )
        y[i], y[4 - i] = odd + even, odd - even
    y[2] = float(D[2, 0]) * o0 + float(D[2, 1]) * o1
    return y


def cross_terms(jump, normal, along):
    t = (LIFT * normal) * jump[along]
    out = [None] * 5
    for f in (0, 4):
        out[f] = t - (LIFT * SPEED) * jump[f]
    for f in (1, 2, 3):
        out[f] = (-LIFT * SPEED) * jump[f]
    g = MACH * jump[1] + jump[0]
    out[along] = out[along] + (LIFT * normal) * g
    return out


def axial_terms(jump, normal):
    p, u, v, w, d = jump
    near = LIFT * (normal * MACH - SPEED)
    t = (LIFT * normal) * u
    return [
        near * p + t,
        near * u + (LIFT * normal) * p,
        (-LIFT * SPEED) * v,
        (-LIFT * SPEED) * w,
        near * d + t,
    ]


def unpack_faces(ref, index, tiles):
    parts = []
    for t in range(tiles):
        wide = ref[index + (slice(16 * t, 16 * t + 16), slice(None))].astype(F32)
        parts += [wide[:8], wide[8:]]
    return parts


def axial_lines(cur, nxt, left, right, b, r, low_half, emit):
    x = [[cur[f, a, b, r] for a in range(5)] for f in range(5)]
    p, u, d = x[0], x[1], x[4]
    diff = {
        0: deriv([MACH * p[a] + u[a] for a in range(5)]),
        1: deriv([MACH * u[a] + p[a] for a in range(5)]),
        4: deriv([MACH * d[a] + u[a] for a in range(5)]),
    }
    jump_lo, jump_hi = [], []
    for f in range(5):
        q = 5 * r + f
        m = q // 2
        if q % 2 == 0:
            halo = jnp.where(low_half, left[m], right[m])
        else:
            halo = pltpu.roll(jnp.where(low_half, right[m], left[m]), 4, 0)
        own = pltpu.roll(jnp.where(low_half, x[f][4], x[f][0]), 4, 0)
        jump_lo.append(x[f][0] - jnp.where(low_half, halo, own))
        jump_hi.append(x[f][4] - jnp.where(low_half, own, halo))
    lo, hi = axial_terms(jump_lo, -1.0), axial_terms(jump_hi, 1.0)
    for a in range(5):
        for f in range(5):
            total = nxt[f, a, b, r]
            if f in diff:
                total = total + diff[f][a]
            if a in (0, 4):
                total = total + (lo[f] if a == 0 else hi[f])
            emit(f, a, total)


def kernel(
    nax, naz,
    state_hbm, lamb_hbm, owner_hbm, element_hbm, class_hbm, table_ref,
    bufs, acc, s_ref, xl, xr,
    q_ref, lamb_ref, owner_ref, element_ref, class_ref, s_acc, post, inbox,
    xs, ys, yl, yr,
    load_sem, mail_send, mail_recv, xsend, xrecv, ysend, yrecv,
):
    n = nax * naz
    groups = n // GROUP
    ax, az = lax.axis_index("ax"), lax.axis_index("az")
    me = ax * naz + az
    has_left, has_right = ax > 0, ax < nax - 1
    az_up, az_down = lax.rem(az + 1, naz), lax.rem(az + naz - 1, naz)
    row = lax.broadcasted_iota(jnp.int32, (8, 128), 0)
    lane = lax.broadcasted_iota(jnp.int32, (8, 128), 1)
    low_half = row < 4
    ey = row & 3

    loads = [
        pltpu.make_async_copy(src, dst, load_sem.at[i])
        for i, (src, dst) in enumerate(
            [(owner_hbm, owner_ref), (element_hbm, element_ref), (class_hbm, class_ref),
             (lamb_hbm, lamb_ref), (state_hbm, q_ref)]
        )
    ]
    for load in loads:
        load.start()

    barrier = pltpu.get_barrier_semaphore()

    def greet(i, carry):
        other = lax.rem(me + i, n)
        pl.semaphore_signal(
            barrier, inc=1, device_id=(other // naz, lax.rem(other, naz)), device_id_type=MESH
        )
        return carry

    lax.fori_loop(1, n, greet, 0)

    @pl.when(jnp.logical_not(has_left))
    def _():
        def body(i, carry):
            for k in range(4):
                xl[k, i] = jnp.zeros(xl.shape[2:], BF16)
            return carry
        lax.fori_loop(0, 5, body, 0)

    @pl.when(jnp.logical_not(has_right))
    def _():
        def body(i, carry):
            for k in range(4):
                xr[k, i] = jnp.zeros(xr.shape[2:], BF16)
            return carry
        lax.fori_loop(0, 5, body, 0)

    for load in loads[:4]:
        load.wait()
    owner, element, shape_class = owner_ref[...], element_ref[...], class_ref[...]
    count = owner.shape[1]
    hit = lax.broadcasted_iota(jnp.int32, (n, count), 0) == owner
    hit = jnp.where(hit, 1.0, 0.0)
    earlier = lax.broadcasted_iota(jnp.int32, (count, count), 0) < lax.broadcasted_iota(
        jnp.int32, (count, count), 1
    )
    ranks = jnp.dot(
        hit.astype(BF16), jnp.where(earlier, 1.0, 0.0).astype(BF16), preferred_element_type=F32
    )
    position = jnp.sum(hit * ranks, axis=0, keepdims=True).astype(jnp.int32)
    values, largest = [], None
    for c in range(3):
        both = lax.dot_general(
            table_ref[...], lamb_ref[c], (((1,), (1,)), ((), ())), preferred_element_type=F32
        )
        value = jnp.where(shape_class == 0, both[:128], both[128:])
        values.append(value)
        top = jnp.max(jnp.abs(value), axis=0, keepdims=True)
        largest = top if largest is None else jnp.maximum(largest, top)
    shift = 14.0 - jnp.floor(jnp.log2(jnp.maximum(largest, 1e-30)))
    gain = jnp.exp2(shift)
    node_row = lax.broadcasted_iota(jnp.int32, (128, count), 0)
    digits = []
    for c in range(3):
        fixed = jnp.clip(jnp.floor(values[c] * gain + 0.5), -32767.0, 32767.0)
        if c == 0:
            fixed = jnp.where(node_row == 125, (element + 1).astype(F32), fixed)
        if c == 1:
            fixed = jnp.where(node_row == 125, shift, fixed)
        high = jnp.floor((fixed + 128.0) * (1.0 / 256.0))
        digits.append([high.astype(BF16), (fixed - 256.0 * high).astype(BF16)])
    slot_row = lax.broadcasted_iota(jnp.int32, (n * 8, count), 0)

    def placed(slot, fields):
        place = jnp.where(slot_row == slot, 1.0, 0.0).astype(BF16)
        out = []
        for c in fields:
            mail = lax.dot_general(
                place, jnp.concatenate(digits[c], axis=0), (((1,), (1,)), ((), ())),
                preferred_element_type=F32,
            )
            out.append((256.0 * mail[:, :128] + mail[:, 128:]).astype(jnp.int32))
        return out

    early = position < 3
    first, second = placed(owner * 8 + position, (0, 1))
    (upper,) = placed(jnp.where(early, owner * 8 + ((position + 6) & 7), -1), (2,))
    (lower,) = placed(jnp.where(early, -1, owner * 8 + ((position + 3) & 7)), (2,))
    pair = ((first << 16) + second).reshape(n, 8, 128)
    third = ((upper << 16) + lower).reshape(n, 8, 128)
    tile_row = lax.broadcasted_iota(jnp.int32, (n, 8, 128), 1)
    post[:, 0:8] = jnp.where(tile_row < 6, pair, third)
    post[:, 8:16] = third

    def x_copy(k, b, side):
        if side == 0:
            dst, dev = xl, (ax + 1, az)
        else:
            dst, dev = xr, (ax - 1, az)
        return pltpu.make_async_remote_copy(
            src_ref=xs.at[k, b, side], dst_ref=dst.at[k, b], send_sem=xsend.at[k, b, side],
            recv_sem=xrecv.at[k, b, side], device_id=dev, device_id_type=MESH,
        )

    def y_copy(k, side):
        if side == 0:
            dst, dev = yl, (ax, az_up)
        else:
            dst, dev = yr, (ax, az_down)
        return pltpu.make_async_remote_copy(
            src_ref=ys.at[k, side], dst_ref=dst.at[k], send_sem=ysend.at[k, side],
            recv_sem=yrecv.at[k, side], device_id=dev, device_id_type=MESH,
        )

    def pack_x(ref, k, b):
        for side in range(2):
            a = 4 if side == 0 else 0
            parts = []
            for m in range(14):
                pair = []
                for q in (2 * m, 2 * m + 1):
                    pair.append(ref[q % 5, a, b, q // 5] if q < 25 else jnp.zeros((8, 128), F32))
                even, odd = pltpu.roll(pair[0], 4, 0), pair[1]
                parts.append(
                    jnp.where(low_half, even, odd) if side == 0 else jnp.where(low_half, odd, even)
                )
            for t in range(7):
                xs[k, b, side, 16 * t:16 * t + 16, :] = jnp.concatenate(
                    [parts[2 * t], parts[2 * t + 1]], axis=0
                ).astype(BF16)

    def pack_y(ref, k, side):
        b = 4 if side == 0 else 0

        def body(a, carry):
            parts = []
            for m in range(8):
                total = jnp.zeros((8, 128), F32)
                for j in range(4):
                    q = 4 * m + j
                    if q < 25:
                        turn = (j - 3) % 8 if side == 0 else (3 + j) % 8
                        value = ref[q % 5, a, b, q // 5]
                        value = pltpu.roll(value, turn, 0) if turn else value
                        residue = j if side == 0 else (3 + j) % 4
                        total = jnp.where(ey == residue, value, total)
                parts.append(total)
            for t in range(4):
                ys[k, side, a, 16 * t:16 * t + 16, :] = jnp.concatenate(
                    [parts[2 * t], parts[2 * t + 1]], axis=0
                ).astype(BF16)
            return carry

        lax.fori_loop(0, 5, body, 0)

    def send_x(k, b):
        @pl.when(has_right)
        def _():
            x_copy(k, b, 0).start()

        @pl.when(has_left)
        def _():
            x_copy(k, b, 1).start()

    def take_x(k, b):
        @pl.when(has_left)
        def _():
            x_copy(k, b, 0).wait_recv()

        @pl.when(has_right)
        def _():
            x_copy(k, b, 1).wait_recv()

    pl.semaphore_wait(barrier, n - 1)

    def mail_out(i, carry):
        other = lax.rem(me + i, n)
        pltpu.make_async_remote_copy(
            src_ref=post.at[other, pl.ds(0, MAIL)], dst_ref=inbox.at[i, pl.ds(0, MAIL)],
            send_sem=mail_send, recv_sem=mail_recv.at[i // GROUP],
            device_id=(other // naz, lax.rem(other, naz)), device_id_type=MESH,
        ).start()
        return carry

    lax.fori_loop(1, n, mail_out, 0)
    inbox[0] = post[me]

    loads[4].wait()
    pack_y(q_ref, 0, 0)
    y_copy(0, 0).start()
    pack_y(q_ref, 0, 1)
    y_copy(0, 1).start()

    def first_x(b, carry):
        pack_x(q_ref, 0, b)
        send_x(0, b)
        return carry

    lax.fori_loop(0, 5, first_x, 0)

    def z_pass(cur, nxt):
        def body(a, carry):
            for b in range(5):
                x = [[cur[f, a, b, r] for r in range(5)] for f in range(5)]
                dw = deriv(x[3])
                dg = deriv([MACH * x[1][r] + x[0][r] for r in range(5)])
                lo = cross_terms(
                    [x[f][0] - jnp.where(lane == 0, 0.0, pltpu.roll(x[f][4], 1, 1)) for f in range(5)],
                    -1.0, 3,
                )
                hi = cross_terms(
                    [x[f][4] - jnp.where(lane == 127, 0.0, pltpu.roll(x[f][0], 127, 1)) for f in range(5)],
                    1.0, 3,
                )
                for r in range(5):
                    for f in range(5):
                        value = dw[r] if f in (0, 4) else dg[r] if f == 3 else None
                        face = lo[f] if r == 0 else hi[f] if r == 4 else None
                        if value is None:
                            value = jnp.zeros((8, 128), F32) if face is None else face
                        elif face is not None:
                            value = value + face
                        nxt[f, a, b, r] = value
            return carry

        lax.fori_loop(0, 5, body, 0)

    def y_pass(cur, nxt, k):
        y_copy(k, 0).wait_recv()
        y_copy(k, 1).wait_recv()

        def body(a, carry):
            down, up = unpack_faces(yl, (k, a), 4), unpack_faces(yr, (k, a), 4)
            for r in range(5):
                x = [[cur[f, a, b, r] for b in range(5)] for f in range(5)]
                dv = deriv(x[2])
                dg = deriv([MACH * x[1][b] + x[0][b] for b in range(5)])
                jump_lo, jump_hi = [], []
                for f in range(5):
                    q = 5 * r + f
                    j = q % 4
                    halo = jnp.where(ey == j, down[q // 4], up[q // 4])
                    halo = pltpu.roll(halo, 8 - j, 0) if j else halo
                    jump_lo.append(x[f][0] - jnp.where(ey == 0, halo, pltpu.roll(x[f][4], 1, 0)))
                    jump_hi.append(x[f][4] - jnp.where(ey == 3, halo, pltpu.roll(x[f][0], 7, 0)))
                lo, hi = cross_terms(jump_lo, -1.0, 2), cross_terms(jump_hi, 1.0, 2)
                for b in range(5):
                    for f in range(5):
                        value = dv[b] if f in (0, 4) else dg[b] if f == 2 else None
                        face = lo[f] if b == 0 else hi[f] if b == 4 else None
                        if value is None and face is None:
                            continue
                        if value is None:
                            value = face
                        elif face is not None:
                            value = value + face
                        nxt[f, a, b, r] = nxt[f, a, b, r] + value
            return carry

        lax.fori_loop(0, 5, body, 0)

    def x_pass(cur, nxt, k, scale, first):
        def body(i, carry):
            b = jnp.where(i == 0, 0, jnp.where(i == 1, 4, i - 1))
            take_x(k, b)
            left, right = unpack_faces(xl, (k, b), 7), unpack_faces(xr, (k, b), 7)
            for r in range(5):
                def emit(f, a, total):
                    if first and f in (1, 2, 3):
                        at = ((f - 1) * 125 + a * 25 + b * 5 + r) * 8
                        total = total + s_ref[pl.ds(pl.multiple_of(at, 8), 8), :]
                    total = scale * total
                    nxt[f, a, b, r] = total
                    before = q_ref[f, a, b, r] if first else acc[f, a, b, r]
                    acc[f, a, b, r] = before + total

                axial_lines(cur, nxt, left, right, b, r, low_half, emit)

            pack_x(nxt, k + 1, b)
            send_x(k + 1, b)

            @pl.when(i == 0)
            def _():
                pack_y(nxt, k + 1, 1)
                y_copy(k + 1, 1).start()

            @pl.when(i == 1)
            def _():
                pack_y(nxt, k + 1, 0)
                y_copy(k + 1, 0).start()
            return carry

        lax.fori_loop(0, 5, body, 0)

    z_pass(q_ref, bufs.at[0])
    y_pass(q_ref, bufs.at[0], 0)

    def mail_block(first_one, many, g):
        return pltpu.make_async_remote_copy(
            src_ref=post.at[pl.ds(first_one, many), pl.ds(0, MAIL)],
            dst_ref=inbox.at[pl.ds(first_one, many), pl.ds(0, MAIL)],
            send_sem=mail_send, recv_sem=mail_recv.at[g],
            device_id=(ax, az), device_id_type=MESH,
        )

    def opened(g):
        block = inbox[pl.ds(g * GROUP, GROUP)]
        upper, lower = block[:, 0:8], block[:, 8:16]
        at = lax.broadcasted_iota(jnp.int32, (GROUP, 8, 128), 1)
        second = (upper << 16) >> 16
        first = (upper - second) >> 16
        third = jnp.where(at >= 6, upper, lower)
        early, late = pltpu.roll(third, 2, 1), pltpu.roll(third, 5, 1)
        third = jnp.where(at < 3, (early - ((early << 16) >> 16)) >> 16, (late << 16) >> 16)
        rows = [
            jnp.where(at < 6, x, 0).astype(F32).reshape(GROUP * 8, 128)
            for x in (first, second, third)
        ]
        code = rows[0][:, 125:126].astype(jnp.int32) - 1
        scale = jnp.exp2(-rows[1][:, 125:126])
        turned = jnp.concatenate([(x * scale).T for x in rows], axis=0)
        high = turned.astype(BF16)
        low = (turned - high.astype(F32)).astype(BF16)
        return code, jnp.concatenate([high, low], axis=1)

    def sums(code, lines, t):
        member = code == lax.broadcasted_iota(jnp.int32, (GROUP * 8, 256), 1) + 256 * t
        member = jnp.where(member, 1.0, 0.0).astype(BF16)
        return jnp.dot(
            lines, jnp.concatenate([member, member], axis=0), preferred_element_type=F32
        )

    def gather_first():
        mail_block(1, GROUP - 1, 0).wait_recv()
        code, lines = opened(0)
        for t in range(4):
            s_acc[:, 256 * t:256 * t + 256] = sums(code, lines, t)

    def gather(g, carry):
        mail_block(g * GROUP, GROUP, g).wait_recv()
        code, lines = opened(g)
        for t in range(4):
            s_acc[:, 256 * t:256 * t + 256] += sums(code, lines, t)
        return carry

    def gather_last():
        mail_block((groups - 1) * GROUP, GROUP, groups - 1).wait_recv()
        code, lines = opened(groups - 1)
        for t in range(4):
            total = s_acc[:, 256 * t:256 * t + 256] + sums(code, lines, t)
            for c in range(3):
                for h in range(2):
                    s_ref[pl.ds(c * 1000 + 2 * t + h, 125, stride=8), :] = total[
                        128 * c:128 * c + 125, 128 * h:128 * h + 128
                    ]

    gather_first()
    lax.fori_loop(1, groups - 1, gather, 0)
    gather_last()

    x_pass(q_ref, bufs.at[0], 0, DT, True)

    def stage(k, carry):
        cur, nxt = bufs.at[lax.rem(k + 1, 2)], bufs.at[lax.rem(k, 2)]
        scale = jnp.where(k == 1, DT / 2.0, DT / 3.0)
        z_pass(cur, nxt)
        y_pass(cur, nxt, k)
        x_pass(cur, nxt, k, scale, False)
        return carry

    lax.fori_loop(1, 3, stage, 0)
    z_pass(bufs.at[0], bufs.at[1])
    y_pass(bufs.at[0], bufs.at[1], 3)

    mail_block(0, n - 1, 0).wait_send()

    def drain(k, carry):
        y_copy(k, 0).wait_send()
        y_copy(k, 1).wait_send()

        def inner(b, carry):
            @pl.when(has_right)
            def _():
                x_copy(k, b, 0).wait_send()

            @pl.when(has_left)
            def _():
                x_copy(k, b, 1).wait_send()
            return carry

        lax.fori_loop(0, 5, inner, 0)
        return carry

    lax.fori_loop(0, 4, drain, 0)
    for b in range(5):
        take_x(3, b)


def finish(bufs, acc, s_ref, xl, xr, new_hbm, source_hbm, new_ref, sem):
    save_source = pltpu.make_async_copy(s_ref, source_hbm, sem.at[5])
    save_source.start()
    low_half = lax.broadcasted_iota(jnp.int32, (8, 128), 0) < 4
    cur, nxt = bufs.at[0], bufs.at[1]

    def save(b):
        return pltpu.make_async_copy(new_ref.at[:, :, b], new_hbm.at[:, :, b], sem.at[b])

    def body(b, carry):
        left, right = unpack_faces(xl, (3, b), 7), unpack_faces(xr, (3, b), 7)
        for r in range(5):
            def emit(f, a, total):
                new_ref[f, a, b, r] = acc[f, a, b, r] + (DT / 4.0) * total

            axial_lines(cur, nxt, left, right, b, r, low_half, emit)
        save(b).start()
        return carry

    lax.fori_loop(0, 5, body, 0)
    for b in range(5):
        save(b).wait()
    save_source.wait()


def body(nax, naz, lamb_vector, owner, element, shape_class, interp_tables, acoustic_state):
    n = nax * naz
    count = lamb_vector.shape[0]
    lamb = jnp.transpose(lamb_vector, (1, 0, 2))
    table = jnp.pad(jnp.transpose(interp_tables, (0, 2, 1)), ((0, 0), (0, 3), (0, 0)))
    table = table.reshape(256, 512)
    nodes = (5, 5, 5, 5, 8, 128)
    state = acoustic_state.reshape(nodes)
    vmem, hbm = pl.BlockSpec(memory_space=pltpu.VMEM), pl.BlockSpec(memory_space=pltpu.HBM)
    dma = pltpu.SemaphoreType.DMA
    kept = pl.pallas_call(
        functools.partial(kernel, nax, naz),
        out_shape=(
            jax.ShapeDtypeStruct((2,) + nodes, F32),
            jax.ShapeDtypeStruct(nodes, F32),
            jax.ShapeDtypeStruct((3000, 128), F32),
            jax.ShapeDtypeStruct((4, 5, 112, 128), BF16),
            jax.ShapeDtypeStruct((4, 5, 112, 128), BF16),
        ),
        in_specs=[hbm] * 5 + [vmem],
        out_specs=(vmem,) * 5,
        scratch_shapes=[
            pltpu.VMEM(nodes, F32),
            pltpu.VMEM(lamb.shape, BF16),
            pltpu.VMEM((1, count), jnp.int32),
            pltpu.VMEM((1, count), jnp.int32),
            pltpu.VMEM((1, count), jnp.int32),
            pltpu.VMEM((384, 1024), F32),
            pltpu.VMEM((n, 16, 128), jnp.int32),
            pltpu.VMEM((n, 16, 128), jnp.int32),
            pltpu.VMEM((4, 5, 2, 112, 128), BF16),
            pltpu.VMEM((4, 2, 5, 64, 128), BF16),
            pltpu.VMEM((4, 5, 64, 128), BF16),
            pltpu.VMEM((4, 5, 64, 128), BF16),
            dma((5,)), dma, dma((n // GROUP,)),
            dma((4, 5, 2)), dma((4, 5, 2)), dma((4, 2)), dma((4, 2)),
        ],
        compiler_params=pltpu.CompilerParams(
            collective_id=0, has_side_effects=True, vmem_limit_bytes=36 * 1024 * 1024
        ),
    )(
        state, lamb,
        owner.reshape(1, count), element.reshape(1, count), shape_class.reshape(1, count), table,
    )
    new, source = pl.pallas_call(
        finish,
        out_shape=(jax.ShapeDtypeStruct(nodes, F32), jax.ShapeDtypeStruct((3000, 128), F32)),
        in_specs=[vmem] * 5,
        out_specs=(hbm, hbm),
        scratch_shapes=[pltpu.VMEM(nodes, F32), dma((6,))],
        compiler_params=pltpu.CompilerParams(vmem_limit_bytes=24 * 1024 * 1024),
    )(*kept)
    return new.reshape(5, 125, 2, 4, 128), source.reshape(3, 125, 2, 4, 128)


def solution(mesh):
    nax, naz = mesh.shape["ax"], mesh.shape["az"]
    in_specs = (
        P(("ax", "az"), None, None),
        P(("ax", "az"), None),
        P(("ax", "az")),
        P(("ax", "az")),
        P(),
        P(None, None, "ax", "az", None),
    )
    out_specs = (P(None, None, "ax", "az", None), P(None, None, "ax", "az", None))
    return jax.shard_map(
        functools.partial(body, nax, naz), mesh=mesh, in_specs=in_specs, out_specs=out_specs,
        check_vma=False,
    )
```

```python
import functools
import math

import jax
import jax.numpy as jnp
import numpy as np
from jax import lax
from jax.experimental import pallas as pl
from jax.experimental.pallas import tpu as pltpu
from jax.sharding import PartitionSpec as P

MACH = 0.3
SPEED = 1.3
DT = 0.03
LIFT = 10.0
VOLUME = 2.0
MAIL = 9
GROUP = 16
MESH = pl.DeviceIdType.MESH
F32 = jnp.float32
BF16 = jnp.bfloat16


def line_matrix():
    points = [-1.0, -math.sqrt(3.0 / 7.0), 0.0, math.sqrt(3.0 / 7.0), 1.0]
    bary = [
        1.0 / math.prod(points[c] - points[o] for o in range(5) if o != c) for c in range(5)
    ]
    d = np.zeros((5, 5))
    for i in range(5):
        for j in range(5):
            if i != j:
                d[i, j] = bary[j] / bary[i] / (points[i] - points[j])
        d[i, i] = -np.sum(d[i])
    return -VOLUME * d


D = line_matrix()


def deriv(x):
    e0, e1, o0, o1 = x[0] + x[4], x[1] + x[3], x[0] - x[4], x[1] - x[3]
    y = [None] * 5
    for i in range(2):
        odd = float(0.5 * (D[i, 0] - D[i, 4])) * o0 + float(0.5 * (D[i, 1] - D[i, 3])) * o1
        even = (
            float(0.5 * (D[i, 0] + D[i, 4])) * e0
            + float(0.5 * (D[i, 1] + D[i, 3])) * e1
            + float(D[i, 2]) * x[2]
        )
        y[i], y[4 - i] = odd + even, odd - even
    y[2] = float(D[2, 0]) * o0 + float(D[2, 1]) * o1
    return y


def cross_terms(jump, normal, along):
    t = (LIFT * normal) * jump[along]
    out = [None] * 5
    for f in (0, 4):
        out[f] = t - (LIFT * SPEED) * jump[f]
    for f in (1, 2, 3):
        out[f] = (-LIFT * SPEED) * jump[f]
    g = MACH * jump[1] + jump[0]
    out[along] = out[along] + (LIFT * normal) * g
    return out


def axial_terms(jump, normal):
    p, u, v, w, d = jump
    near = LIFT * (normal * MACH - SPEED)
    t = (LIFT * normal) * u
    return [
        near * p + t,
        near * u + (LIFT * normal) * p,
        (-LIFT * SPEED) * v,
        (-LIFT * SPEED) * w,
        near * d + t,
    ]


def unpack_faces(ref, index, tiles):
    parts = []
    for t in range(tiles):
        wide = ref[index + (slice(16 * t, 16 * t + 16), slice(None))].astype(F32)
        parts += [wide[:8], wide[8:]]
    return parts


def axial_lines(cur, nxt, left, right, b, r, low_half, emit):
    x = [[cur[f, a, b, r] for a in range(5)] for f in range(5)]
    p, u, d = x[0], x[1], x[4]
    diff = {
        0: deriv([MACH * p[a] + u[a] for a in range(5)]),
        1: deriv([MACH * u[a] + p[a] for a in range(5)]),
        4: deriv([MACH * d[a] + u[a] for a in range(5)]),
    }
    jump_lo, jump_hi = [], []
    for f in range(5):
        q = 5 * r + f
        m = q // 2
        if q % 2 == 0:
            halo = jnp.where(low_half, left[m], right[m])
        else:
            halo = pltpu.roll(jnp.where(low_half, right[m], left[m]), 4, 0)
        own = pltpu.roll(jnp.where(low_half, x[f][4], x[f][0]), 4, 0)
        jump_lo.append(x[f][0] - jnp.where(low_half, halo, own))
        jump_hi.append(x[f][4] - jnp.where(low_half, own, halo))
    lo, hi = axial_terms(jump_lo, -1.0), axial_terms(jump_hi, 1.0)
    for a in range(5):
        for f in range(5):
            total = nxt[f, a, b, r]
            if f in diff:
                total = total + diff[f][a]
            if a in (0, 4):
                total = total + (lo[f] if a == 0 else hi[f])
            emit(f, a, total)


def kernel(
    nax, naz,
    state_hbm, lamb_hbm, key_ref, table_ref,
    even, odd, acc, s_ref, xl, xr,
    lamb_ref, s_acc, post, inbox,
    xs, ys, yl, yr,
    load_sem, mail_send, mail_recv, xsend, xrecv, ysend, yrecv,
):
    n = nax * naz
    groups = n // GROUP
    ax, az = lax.axis_index("ax"), lax.axis_index("az")
    me = ax * naz + az
    has_left, has_right = ax > 0, ax < nax - 1
    az_up, az_down = lax.rem(az + 1, naz), lax.rem(az + naz - 1, naz)
    row = lax.broadcasted_iota(jnp.int32, (8, 128), 0)
    lane = lax.broadcasted_iota(jnp.int32, (8, 128), 1)
    low_half = row < 4
    ey = row & 3

    loads = [
        pltpu.make_async_copy(src, dst, load_sem.at[i])
        for i, (src, dst) in enumerate(
            [(lamb_hbm, lamb_ref), (state_hbm, even), (state_hbm, acc)]
        )
    ]
    for load in loads:
        load.start()

    barrier = pltpu.get_barrier_semaphore()

    def greet(i, carry):
        other = lax.rem(me + i, n)
        pl.semaphore_signal(
            barrier, inc=1, device_id=(other // naz, lax.rem(other, naz)), device_id_type=MESH
        )
        return carry

    lax.fori_loop(1, n, greet, 0)

    @pl.when(jnp.logical_not(has_left))
    def _():
        def body(i, carry):
            for k in range(4):
                xl[k, i] = jnp.zeros(xl.shape[2:], BF16)
            return carry
        lax.fori_loop(0, 5, body, 0)

    @pl.when(jnp.logical_not(has_right))
    def _():
        def body(i, carry):
            for k in range(4):
                xr[k, i] = jnp.zeros(xr.shape[2:], BF16)
            return carry
        lax.fori_loop(0, 5, body, 0)

    key = key_ref[...]
    owner, element, shape_class = lax.rem(key, n), (key // n) >> 1, (key // n) & 1
    count = owner.shape[1]
    hit = lax.broadcasted_iota(jnp.int32, (n, count), 0) == owner
    hit = jnp.where(hit, 1.0, 0.0)
    earlier = lax.broadcasted_iota(jnp.int32, (count, count), 0) < lax.broadcasted_iota(
        jnp.int32, (count, count), 1
    )
    ranks = jnp.dot(
        hit.astype(BF16), jnp.where(earlier, 1.0, 0.0).astype(BF16), preferred_element_type=F32
    )
    position = jnp.sum(hit * ranks, axis=0, keepdims=True).astype(jnp.int32)
    values, largest = [], None
    loads[0].wait()
    for c in range(3):
        both = lax.dot_general(
            table_ref[...], lamb_ref[c], (((1,), (1,)), ((), ())), preferred_element_type=F32
        )
        value = jnp.where(shape_class == 0, both[:128], both[128:])
        values.append(value)
        top = jnp.max(jnp.abs(value), axis=0, keepdims=True)
        largest = top if largest is None else jnp.maximum(largest, top)
    shift = 14.0 - jnp.floor(jnp.log2(jnp.maximum(largest, 1e-30)))
    gain = jnp.exp2(shift)
    node_row = lax.broadcasted_iota(jnp.int32, (128, count), 0)
    digits = []
    for c in range(3):
        fixed = jnp.clip(jnp.floor(values[c] * gain + 0.5), -32767.0, 32767.0)
        if c == 0:
            fixed = jnp.where(node_row == 125, (element + 1).astype(F32), fixed)
        if c == 1:
            fixed = jnp.where(node_row == 125, shift, fixed)
        high = jnp.floor((fixed + 128.0) * (1.0 / 256.0))
        digits.append([high.astype(BF16), (fixed - 256.0 * high).astype(BF16)])
    slot_row = lax.broadcasted_iota(jnp.int32, (n * 8, count), 0)

    def placed(slot, fields):
        place = jnp.where(slot_row == slot, 1.0, 0.0).astype(BF16)
        out = []
        for c in fields:
            mail = lax.dot_general(
                place, jnp.concatenate(digits[c], axis=0), (((1,), (1,)), ((), ())),
                preferred_element_type=F32,
            )
            out.append((256.0 * mail[:, :128] + mail[:, 128:]).astype(jnp.int32))
        return out

    early = position < 3
    first, second = placed(owner * 8 + position, (0, 1))
    (upper,) = placed(jnp.where(early, owner * 8 + ((position + 6) & 7), -1), (2,))
    (lower,) = placed(jnp.where(early, -1, owner * 8 + ((position + 3) & 7)), (2,))
    pair = ((first << 16) + second).reshape(n, 8, 128)
    third = ((upper << 16) + lower).reshape(n, 8, 128)
    tile_row = lax.broadcasted_iota(jnp.int32, (n, 8, 128), 1)
    post[:, 0:8] = jnp.where(tile_row < 6, pair, third)
    post[:, 8:16] = third

    def x_copy(k, b, side):
        if side == 0:
            dst, dev = xl, (ax + 1, az)
        else:
            dst, dev = xr, (ax - 1, az)
        return pltpu.make_async_remote_copy(
            src_ref=xs.at[k, b, side], dst_ref=dst.at[k, b], send_sem=xsend.at[k, b, side],
            recv_sem=xrecv.at[k, b, side], device_id=dev, device_id_type=MESH,
        )

    def y_copy(k, side):
        if side == 0:
            dst, dev = yl, (ax, az_up)
        else:
            dst, dev = yr, (ax, az_down)
        return pltpu.make_async_remote_copy(
            src_ref=ys.at[k, side], dst_ref=dst.at[k], send_sem=ysend.at[k, side],
            recv_sem=yrecv.at[k, side], device_id=dev, device_id_type=MESH,
        )

    def pack_x(ref, k, b):
        for side in range(2):
            a = 4 if side == 0 else 0
            parts = []
            for m in range(14):
                pair = []
                for q in (2 * m, 2 * m + 1):
                    pair.append(ref[q % 5, a, b, q // 5] if q < 25 else jnp.zeros((8, 128), F32))
                even, odd = pltpu.roll(pair[0], 4, 0), pair[1]
                parts.append(
                    jnp.where(low_half, even, odd) if side == 0 else jnp.where(low_half, odd, even)
                )
            for t in range(7):
                xs[k, b, side, 16 * t:16 * t + 16, :] = jnp.concatenate(
                    [parts[2 * t], parts[2 * t + 1]], axis=0
                ).astype(BF16)

    def pack_y(ref, k, side):
        b = 4 if side == 0 else 0

        def body(a, carry):
            parts = []
            for m in range(8):
                total = jnp.zeros((8, 128), F32)
                for j in range(4):
                    q = 4 * m + j
                    if q < 25:
                        turn = (j - 3) % 8 if side == 0 else (3 + j) % 8
                        value = ref[q % 5, a, b, q // 5]
                        value = pltpu.roll(value, turn, 0) if turn else value
                        residue = j if side == 0 else (3 + j) % 4
                        total = jnp.where(ey == residue, value, total)
                parts.append(total)
            for t in range(4):
                ys[k, side, a, 16 * t:16 * t + 16, :] = jnp.concatenate(
                    [parts[2 * t], parts[2 * t + 1]], axis=0
                ).astype(BF16)
            return carry

        lax.fori_loop(0, 5, body, 0)

    def send_x(k, b):
        @pl.when(has_right)
        def _():
            x_copy(k, b, 0).start()

        @pl.when(has_left)
        def _():
            x_copy(k, b, 1).start()

    def take_x(k, b):
        @pl.when(has_left)
        def _():
            x_copy(k, b, 0).wait_recv()

        @pl.when(has_right)
        def _():
            x_copy(k, b, 1).wait_recv()

    pl.semaphore_wait(barrier, n - 1)

    def mail_out(i, carry):
        other = lax.rem(me + i, n)
        pltpu.make_async_remote_copy(
            src_ref=post.at[other, pl.ds(0, MAIL)], dst_ref=inbox.at[i, pl.ds(0, MAIL)],
            send_sem=mail_send, recv_sem=mail_recv.at[i // GROUP],
            device_id=(other // naz, lax.rem(other, naz)), device_id_type=MESH,
        ).start()
        return carry

    lax.fori_loop(1, n, mail_out, 0)
    inbox[0] = post[me]

    loads[1].wait()
    pack_y(even, 0, 0)
    y_copy(0, 0).start()
    pack_y(even, 0, 1)
    y_copy(0, 1).start()

    def first_x(b, carry):
        pack_x(even, 0, b)
        send_x(0, b)
        return carry

    lax.fori_loop(0, 5, first_x, 0)
    loads[2].wait()

    def z_pass(cur, nxt):
        def body(a, carry):
            for b in range(5):
                x = [[cur[f, a, b, r] for r in range(5)] for f in range(5)]
                dw = deriv(x[3])
                dg = deriv([MACH * x[1][r] + x[0][r] for r in range(5)])
                lo = cross_terms(
                    [x[f][0] - jnp.where(lane == 0, 0.0, pltpu.roll(x[f][4], 1, 1)) for f in range(5)],
                    -1.0, 3,
                )
                hi = cross_terms(
                    [x[f][4] - jnp.where(lane == 127, 0.0, pltpu.roll(x[f][0], 127, 1)) for f in range(5)],
                    1.0, 3,
                )
                for r in range(5):
                    for f in range(5):
                        value = dw[r] if f in (0, 4) else dg[r] if f == 3 else None
                        face = lo[f] if r == 0 else hi[f] if r == 4 else None
                        if value is None:
                            value = jnp.zeros((8, 128), F32) if face is None else face
                        elif face is not None:
                            value = value + face
                        nxt[f, a, b, r] = value
            return carry

        lax.fori_loop(0, 5, body, 0)

    def y_pass(cur, nxt):
        def body(a, carry):
            for r in range(5):
                x = [[cur[f, a, b, r] for b in range(5)] for f in range(5)]
                dv = deriv(x[2])
                dg = deriv([MACH * x[1][b] + x[0][b] for b in range(5)])
                jump_lo, jump_hi = [], []
                for f in range(5):
                    jump_lo.append(x[f][0] - jnp.where(ey == 0, 0.0, pltpu.roll(x[f][4], 1, 0)))
                    jump_hi.append(x[f][4] - jnp.where(ey == 3, 0.0, pltpu.roll(x[f][0], 7, 0)))
                lo, hi = cross_terms(jump_lo, -1.0, 2), cross_terms(jump_hi, 1.0, 2)
                ready = []
                for b in range(5):
                    for f in range(5):
                        value = dv[b] if f in (0, 4) else dg[b] if f == 2 else None
                        face = lo[f] if b == 0 else hi[f] if b == 4 else None
                        if value is None and face is None:
                            continue
                        if value is None:
                            value = face
                        elif face is not None:
                            value = value + face
                        ready.append((f, b, nxt[f, a, b, r] + value))
                for f, b, value in ready:
                    nxt[f, a, b, r] = value
            return carry

        lax.fori_loop(0, 5, body, 0)

    def y_fix(nxt, k, side):
        b, normal, edge = (0, -1.0, 0) if side == 0 else (4, 1.0, 3)
        y_copy(k, side).wait_recv()

        def body(a, carry):
            faces = unpack_faces(yl if side == 0 else yr, (k, a), 4)
            for r in range(5):
                jump = []
                for f in range(5):
                    q = 5 * r + f
                    j = q % 4
                    halo = pltpu.roll(faces[q // 4], 8 - j, 0) if j else faces[q // 4]
                    jump.append(jnp.where(ey == edge, -halo, 0.0))
                ready = [nxt[f, a, b, r] + t for f, t in enumerate(cross_terms(jump, normal, 2))]
                for f in range(5):
                    nxt[f, a, b, r] = ready[f]
            return carry

        lax.fori_loop(0, 5, body, 0)

    def x_pass(cur, nxt, k, scale):
        def body(i, carry):
            b = jnp.where(i == 3, 0, jnp.where(i == 4, 4, i + 1))

            @pl.when(i == 3)
            def _():
                y_fix(nxt, k, 0)

            @pl.when(i == 4)
            def _():
                y_fix(nxt, k, 1)

            take_x(k, b)
            left, right = unpack_faces(xl, (k, b), 7), unpack_faces(xr, (k, b), 7)
            for r in range(5):
                def emit(f, a, total):
                    total = scale * total
                    nxt[f, a, b, r] = total
                    acc[f, a, b, r] = acc[f, a, b, r] + total

                axial_lines(cur, nxt, left, right, b, r, low_half, emit)

            pack_x(nxt, k + 1, b)
            send_x(k + 1, b)

            @pl.when(i == 3)
            def _():
                pack_y(nxt, k + 1, 1)
                y_copy(k + 1, 1).start()

            @pl.when(i == 4)
            def _():
                pack_y(nxt, k + 1, 0)
                y_copy(k + 1, 0).start()
            return carry

        lax.fori_loop(0, 5, body, 0)

    def mail_block(first_one, many, g):
        return pltpu.make_async_remote_copy(
            src_ref=post.at[pl.ds(first_one, many), pl.ds(0, MAIL)],
            dst_ref=inbox.at[pl.ds(first_one, many), pl.ds(0, MAIL)],
            send_sem=mail_send, recv_sem=mail_recv.at[g],
            device_id=(ax, az), device_id_type=MESH,
        )

    def opened(g):
        block = inbox[pl.ds(g * GROUP, GROUP)]
        upper, lower = block[:, 0:8], block[:, 8:16]
        at = lax.broadcasted_iota(jnp.int32, (GROUP, 8, 128), 1)
        second = (upper << 16) >> 16
        first = (upper - second) >> 16
        third = jnp.where(at >= 6, upper, lower)
        early, late = pltpu.roll(third, 2, 1), pltpu.roll(third, 5, 1)
        third = jnp.where(at < 3, (early - ((early << 16) >> 16)) >> 16, (late << 16) >> 16)
        rows = [
            jnp.where(at < 6, x, 0).astype(F32).reshape(GROUP * 8, 128)
            for x in (first, second, third)
        ]
        code = rows[0][:, 125:126].astype(jnp.int32) - 1
        scale = jnp.exp2(-rows[1][:, 125:126])
        turned = jnp.concatenate([(x * scale).T for x in rows], axis=0)
        high = turned.astype(BF16)
        low = (turned - high.astype(F32)).astype(BF16)
        return code, jnp.concatenate([high, low], axis=1)

    def sums(code, lines, t):
        member = code == lax.broadcasted_iota(jnp.int32, (GROUP * 8, 256), 1) + 256 * t
        member = jnp.where(member, 1.0, 0.0).astype(BF16)
        return jnp.dot(
            lines, jnp.concatenate([member, member], axis=0), preferred_element_type=F32
        )

    def gather_first():
        mail_block(1, GROUP - 1, 0).wait_recv()
        code, lines = opened(0)
        for t in range(4):
            s_acc[:, 256 * t:256 * t + 256] = sums(code, lines, t)

    def gather(g, carry):
        mail_block(g * GROUP, GROUP, g).wait_recv()
        code, lines = opened(g)
        for t in range(4):
            s_acc[:, 256 * t:256 * t + 256] += sums(code, lines, t)
        return carry

    def gather_last():
        mail_block((groups - 1) * GROUP, GROUP, groups - 1).wait_recv()
        code, lines = opened(groups - 1)
        for t in range(4):
            total = s_acc[:, 256 * t:256 * t + 256] + sums(code, lines, t)
            for c in range(3):
                for h in range(2):
                    s_ref[pl.ds(c * 1000 + 2 * t + h, 125, stride=8), :] = total[
                        128 * c:128 * c + 125, 128 * h:128 * h + 128
                    ]

    def add_source(nxt):
        def body(i, carry):
            for j in range(25):
                a, b, r = i, j // 5, j % 5
                for c in range(3):
                    at = (c * 125 + i * 25 + j) * 8
                    nxt[c + 1, a, b, r] = (
                        nxt[c + 1, a, b, r] + s_ref[pl.ds(pl.multiple_of(at, 8), 8), :]
                    )
            return carry

        lax.fori_loop(0, 5, body, 0)

    for k in range(4):
        cur, nxt = (even, odd) if k % 2 == 0 else (odd, even)
        z_pass(cur, nxt)
        y_pass(cur, nxt)
        if k == 0:
            gather_first()
            lax.fori_loop(1, groups - 1, gather, 0)
            gather_last()
            add_source(nxt)
        if k < 3:
            x_pass(cur, nxt, k, DT / (k + 1))

    mail_block(0, n - 1, 0).wait_send()

    def drain(k, carry):
        y_copy(k, 0).wait_send()
        y_copy(k, 1).wait_send()

        def inner(b, carry):
            @pl.when(has_right)
            def _():
                x_copy(k, b, 0).wait_send()

            @pl.when(has_left)
            def _():
                x_copy(k, b, 1).wait_send()
            return carry

        lax.fori_loop(0, 5, inner, 0)
        return carry

    lax.fori_loop(0, 4, drain, 0)
    y_fix(even, 3, 0)
    y_fix(even, 3, 1)
    for b in range(5):
        take_x(3, b)


def finish(nxt, cur, acc, s_ref, xl, xr, new_hbm, source_hbm, new_ref, sem):
    save_source = pltpu.make_async_copy(s_ref, source_hbm, sem.at[5])
    save_source.start()
    low_half = lax.broadcasted_iota(jnp.int32, (8, 128), 0) < 4

    def save(b):
        return pltpu.make_async_copy(new_ref.at[:, :, b], new_hbm.at[:, :, b], sem.at[b])

    def body(b, carry):
        left, right = unpack_faces(xl, (3, b), 7), unpack_faces(xr, (3, b), 7)
        for r in range(5):
            def emit(f, a, total):
                new_ref[f, a, b, r] = acc[f, a, b, r] + (DT / 4.0) * total

            axial_lines(cur, nxt, left, right, b, r, low_half, emit)
        save(b).start()
        return carry

    lax.fori_loop(0, 5, body, 0)
    for b in range(5):
        save(b).wait()
    save_source.wait()


def body(nax, naz, lamb_vector, owner, element, shape_class, interp_tables, acoustic_state):
    n = nax * naz
    count = lamb_vector.shape[0]
    lamb = jnp.transpose(lamb_vector, (1, 0, 2))
    table = jnp.pad(jnp.transpose(interp_tables, (0, 2, 1)), ((0, 0), (0, 3), (0, 0)))
    table = table.reshape(256, 512)
    nodes = (5, 5, 5, 5, 8, 128)
    state = acoustic_state.reshape(nodes)
    key = ((element * 2 + shape_class) * n + owner[:, 0]).reshape(1, count)
    vmem, hbm = pl.BlockSpec(memory_space=pltpu.VMEM), pl.BlockSpec(memory_space=pltpu.HBM)
    dma = pltpu.SemaphoreType.DMA
    kept = pl.pallas_call(
        functools.partial(kernel, nax, naz),
        out_shape=(
            jax.ShapeDtypeStruct(nodes, F32),
            jax.ShapeDtypeStruct(nodes, F32),
            jax.ShapeDtypeStruct(nodes, F32),
            jax.ShapeDtypeStruct((3000, 128), F32),
            jax.ShapeDtypeStruct((4, 5, 112, 128), BF16),
            jax.ShapeDtypeStruct((4, 5, 112, 128), BF16),
        ),
        in_specs=[hbm, hbm, vmem, vmem],
        out_specs=(vmem,) * 6,
        scratch_shapes=[
            pltpu.VMEM(lamb.shape, BF16),
            pltpu.VMEM((384, 1024), F32),
            pltpu.VMEM((n, 16, 128), jnp.int32),
            pltpu.VMEM((n, 16, 128), jnp.int32),
            pltpu.VMEM((4, 5, 2, 112, 128), BF16),
            pltpu.VMEM((4, 2, 5, 64, 128), BF16),
            pltpu.VMEM((4, 5, 64, 128), BF16),
            pltpu.VMEM((4, 5, 64, 128), BF16),
            dma((3,)), dma, dma((n // GROUP,)),
            dma((4, 5, 2)), dma((4, 5, 2)), dma((4, 2)), dma((4, 2)),
        ],
        compiler_params=pltpu.CompilerParams(
            collective_id=0, has_side_effects=True, vmem_limit_bytes=36 * 1024 * 1024
        ),
    )(state, lamb, key, table)
    new, source = pl.pallas_call(
        finish,
        out_shape=(jax.ShapeDtypeStruct(nodes, F32), jax.ShapeDtypeStruct((3000, 128), F32)),
        in_specs=[vmem] * 6,
        out_specs=(hbm, hbm),
        scratch_shapes=[pltpu.VMEM(nodes, F32), dma((6,))],
        compiler_params=pltpu.CompilerParams(vmem_limit_bytes=24 * 1024 * 1024),
    )(*kept)
    return new.reshape(5, 125, 2, 4, 128), source.reshape(3, 125, 2, 4, 128)


def solution(mesh):
    nax, naz = mesh.shape["ax"], mesh.shape["az"]
    in_specs = (
        P(("ax", "az"), None, None),
        P(("ax", "az"), None),
        P(("ax", "az")),
        P(("ax", "az")),
        P(),
        P(None, None, "ax", "az", None),
    )
    out_specs = (P(None, None, "ax", "az", None), P(None, None, "ax", "az", None))
    return jax.shard_map(
        functools.partial(body, nax, naz), mesh=mesh, in_specs=in_specs, out_specs=out_specs,
        check_vma=False,
    )
```

```python
import functools
import math

import jax
import jax.numpy as jnp
import numpy as np
from jax import lax
from jax.experimental import pallas as pl
from jax.experimental.pallas import tpu as pltpu
from jax.sharding import PartitionSpec as P

MACH = 0.3
SPEED = 1.3
DT = 0.03
LIFT = 10.0
VOLUME = 2.0
MAIL = 9
GROUP = 16
MESH = pl.DeviceIdType.MESH
F32 = jnp.float32
BF16 = jnp.bfloat16


def line_matrix():
    points = [-1.0, -math.sqrt(3.0 / 7.0), 0.0, math.sqrt(3.0 / 7.0), 1.0]
    bary = [
        1.0 / math.prod(points[c] - points[o] for o in range(5) if o != c) for c in range(5)
    ]
    d = np.zeros((5, 5))
    for i in range(5):
        for j in range(5):
            if i != j:
                d[i, j] = bary[j] / bary[i] / (points[i] - points[j])
        d[i, i] = -np.sum(d[i])
    return -VOLUME * d


D = line_matrix()


def deriv(x):
    e0, e1, o0, o1 = x[0] + x[4], x[1] + x[3], x[0] - x[4], x[1] - x[3]
    y = [None] * 5
    for i in range(2):
        odd = float(0.5 * (D[i, 0] - D[i, 4])) * o0 + float(0.5 * (D[i, 1] - D[i, 3])) * o1
        even = (
            float(0.5 * (D[i, 0] + D[i, 4])) * e0
            + float(0.5 * (D[i, 1] + D[i, 3])) * e1
            + float(D[i, 2]) * x[2]
        )
        y[i], y[4 - i] = odd + even, odd - even
    y[2] = float(D[2, 0]) * o0 + float(D[2, 1]) * o1
    return y


def cross_terms(jump, normal, along):
    t = (LIFT * normal) * jump[along]
    out = [None] * 5
    for f in (0, 4):
        out[f] = t - (LIFT * SPEED) * jump[f]
    for f in (1, 2, 3):
        out[f] = (-LIFT * SPEED) * jump[f]
    g = MACH * jump[1] + jump[0]
    out[along] = out[along] + (LIFT * normal) * g
    return out


def axial_terms(jump, normal):
    p, u, v, w, d = jump
    near = LIFT * (normal * MACH - SPEED)
    t = (LIFT * normal) * u
    return [
        near * p + t,
        near * u + (LIFT * normal) * p,
        (-LIFT * SPEED) * v,
        (-LIFT * SPEED) * w,
        near * d + t,
    ]


def unpack_faces(ref, index, tiles):
    parts = []
    for t in range(tiles):
        wide = ref[index + (slice(16 * t, 16 * t + 16), slice(None))].astype(F32)
        parts += [wide[:8], wide[8:]]
    return parts


def axial_lines(cur, nxt, left, right, b, r, low_half, emit):
    x = [[cur[f, a, b, r] for a in range(5)] for f in range(5)]
    p, u, d = x[0], x[1], x[4]
    diff = {
        0: deriv([MACH * p[a] + u[a] for a in range(5)]),
        1: deriv([MACH * u[a] + p[a] for a in range(5)]),
        4: deriv([MACH * d[a] + u[a] for a in range(5)]),
    }
    jump_lo, jump_hi = [], []
    for f in range(5):
        q = 5 * r + f
        m = q // 2
        if q % 2 == 0:
            halo = jnp.where(low_half, left[m], right[m])
        else:
            halo = pltpu.roll(jnp.where(low_half, right[m], left[m]), 4, 0)
        own = pltpu.roll(jnp.where(low_half, x[f][4], x[f][0]), 4, 0)
        jump_lo.append(x[f][0] - jnp.where(low_half, halo, own))
        jump_hi.append(x[f][4] - jnp.where(low_half, own, halo))
    lo, hi = axial_terms(jump_lo, -1.0), axial_terms(jump_hi, 1.0)
    for a in range(5):
        for f in range(5):
            total = nxt[f, a, b, r]
            if f in diff:
                total = total + diff[f][a]
            if a in (0, 4):
                total = total + (lo[f] if a == 0 else hi[f])
            emit(f, a, total)


def kernel(
    nax, naz,
    state_hbm, lamb_hbm, key_ref, table_ref,
    even, odd, acc, s_ref, xl, xr,
    lamb_ref, s_acc, post, inbox,
    xs, ys, yl, yr,
    load_sem, mail_send, mail_recv, xsend, xrecv, ysend, yrecv,
):
    n = nax * naz
    groups = n // GROUP
    ax, az = lax.axis_index("ax"), lax.axis_index("az")
    me = ax * naz + az
    has_left, has_right = ax > 0, ax < nax - 1
    az_up, az_down = lax.rem(az + 1, naz), lax.rem(az + naz - 1, naz)
    row = lax.broadcasted_iota(jnp.int32, (8, 128), 0)
    lane = lax.broadcasted_iota(jnp.int32, (8, 128), 1)
    low_half = row < 4
    ey = row & 3

    loads = [
        pltpu.make_async_copy(src, dst, load_sem.at[i])
        for i, (src, dst) in enumerate(
            [(lamb_hbm, lamb_ref), (state_hbm, even), (state_hbm, acc)]
        )
    ]
    for load in loads:
        load.start()

    barrier = pltpu.get_barrier_semaphore()

    def greet(i, carry):
        other = lax.rem(me + i, n)
        pl.semaphore_signal(
            barrier, inc=1, device_id=(other // naz, lax.rem(other, naz)), device_id_type=MESH
        )
        return carry

    lax.fori_loop(1, n, greet, 0)

    @pl.when(jnp.logical_not(has_left))
    def _():
        def body(i, carry):
            for k in range(4):
                xl[k, i] = jnp.zeros(xl.shape[2:], BF16)
            return carry
        lax.fori_loop(0, 5, body, 0)

    @pl.when(jnp.logical_not(has_right))
    def _():
        def body(i, carry):
            for k in range(4):
                xr[k, i] = jnp.zeros(xr.shape[2:], BF16)
            return carry
        lax.fori_loop(0, 5, body, 0)

    key = key_ref[...]
    owner, element, shape_class = lax.rem(key, n), (key // n) >> 1, (key // n) & 1
    count = owner.shape[1]
    hit = lax.broadcasted_iota(jnp.int32, (n, count), 0) == owner
    hit = jnp.where(hit, 1.0, 0.0)
    earlier = lax.broadcasted_iota(jnp.int32, (count, count), 0) < lax.broadcasted_iota(
        jnp.int32, (count, count), 1
    )
    ranks = jnp.dot(
        hit.astype(BF16), jnp.where(earlier, 1.0, 0.0).astype(BF16), preferred_element_type=F32
    )
    position = jnp.sum(hit * ranks, axis=0, keepdims=True).astype(jnp.int32)
    values, largest = [], None
    loads[0].wait()
    for c in range(3):
        both = lax.dot_general(
            table_ref[...], lamb_ref[c], (((1,), (1,)), ((), ())), preferred_element_type=F32
        )
        value = jnp.where(shape_class == 0, both[:128], both[128:])
        values.append(value)
        top = jnp.max(jnp.abs(value), axis=0, keepdims=True)
        largest = top if largest is None else jnp.maximum(largest, top)
    shift = 14.0 - jnp.floor(jnp.log2(jnp.maximum(largest, 1e-30)))
    gain = jnp.exp2(shift)
    node_row = lax.broadcasted_iota(jnp.int32, (128, count), 0)
    digits = []
    for c in range(3):
        fixed = jnp.clip(jnp.floor(values[c] * gain + 0.5), -32767.0, 32767.0)
        if c == 0:
            fixed = jnp.where(node_row == 125, (element + 1).astype(F32), fixed)
        if c == 1:
            fixed = jnp.where(node_row == 125, shift, fixed)
        high = jnp.floor((fixed + 128.0) * (1.0 / 256.0))
        digits.append([high.astype(BF16), (fixed - 256.0 * high).astype(BF16)])
    slot_row = lax.broadcasted_iota(jnp.int32, (n * 8, count), 0)

    def placed(slot, fields):
        place = jnp.where(slot_row == slot, 1.0, 0.0).astype(BF16)
        out = []
        for c in fields:
            mail = lax.dot_general(
                place, jnp.concatenate(digits[c], axis=0), (((1,), (1,)), ((), ())),
                preferred_element_type=F32,
            )
            out.append((256.0 * mail[:, :128] + mail[:, 128:]).astype(jnp.int32))
        return out

    early = position < 3
    first, second = placed(owner * 8 + position, (0, 1))
    (upper,) = placed(jnp.where(early, owner * 8 + ((position + 6) & 7), -1), (2,))
    (lower,) = placed(jnp.where(early, -1, owner * 8 + ((position + 3) & 7)), (2,))
    pair = ((first << 16) + second).reshape(n, 8, 128)
    third = ((upper << 16) + lower).reshape(n, 8, 128)
    tile_row = lax.broadcasted_iota(jnp.int32, (n, 8, 128), 1)
    post[:, 0:8] = jnp.where(tile_row < 6, pair, third)
    post[:, 8:16] = third

    def x_copy(k, b, side):
        if side == 0:
            dst, dev = xl, (ax + 1, az)
        else:
            dst, dev = xr, (ax - 1, az)
        return pltpu.make_async_remote_copy(
            src_ref=xs.at[k, b, side], dst_ref=dst.at[k, b], send_sem=xsend.at[k, b, side],
            recv_sem=xrecv.at[k, b, side], device_id=dev, device_id_type=MESH,
        )

    def y_copy(k, side):
        if side == 0:
            dst, dev = yl, (ax, az_up)
        else:
            dst, dev = yr, (ax, az_down)
        return pltpu.make_async_remote_copy(
            src_ref=ys.at[k, side], dst_ref=dst.at[k], send_sem=ysend.at[k, side],
            recv_sem=yrecv.at[k, side], device_id=dev, device_id_type=MESH,
        )

    def pack_x(ref, k, b):
        for side in range(2):
            a = 4 if side == 0 else 0
            parts = []
            for m in range(14):
                pair = []
                for q in (2 * m, 2 * m + 1):
                    pair.append(ref[q % 5, a, b, q // 5] if q < 25 else jnp.zeros((8, 128), F32))
                even, odd = pltpu.roll(pair[0], 4, 0), pair[1]
                parts.append(
                    jnp.where(low_half, even, odd) if side == 0 else jnp.where(low_half, odd, even)
                )
            for t in range(7):
                xs[k, b, side, 16 * t:16 * t + 16, :] = jnp.concatenate(
                    [parts[2 * t], parts[2 * t + 1]], axis=0
                ).astype(BF16)

    def pack_y(ref, k, side):
        b = 4 if side == 0 else 0

        def body(a, carry):
            parts = []
            for m in range(8):
                total = jnp.zeros((8, 128), F32)
                for j in range(4):
                    q = 4 * m + j
                    if q < 25:
                        turn = (j - 3) % 8 if side == 0 else (3 + j) % 8
                        value = ref[q % 5, a, b, q // 5]
                        value = pltpu.roll(value, turn, 0) if turn else value
                        residue = j if side == 0 else (3 + j) % 4
                        total = jnp.where(ey == residue, value, total)
                parts.append(total)
            for t in range(4):
                ys[k, side, a, 16 * t:16 * t + 16, :] = jnp.concatenate(
                    [parts[2 * t], parts[2 * t + 1]], axis=0
                ).astype(BF16)
            return carry

        lax.fori_loop(0, 5, body, 0)

    def send_x(k, b):
        @pl.when(has_right)
        def _():
            x_copy(k, b, 0).start()

        @pl.when(has_left)
        def _():
            x_copy(k, b, 1).start()

    def take_x(k, b):
        @pl.when(has_left)
        def _():
            x_copy(k, b, 0).wait_recv()

        @pl.when(has_right)
        def _():
            x_copy(k, b, 1).wait_recv()

    pl.semaphore_wait(barrier, n - 1)

    def mail_out(i, carry):
        other = lax.rem(me + 37 * i, n)
        pltpu.make_async_remote_copy(
            src_ref=post.at[other, pl.ds(0, MAIL)], dst_ref=inbox.at[i, pl.ds(0, MAIL)],
            send_sem=mail_send, recv_sem=mail_recv.at[i // GROUP],
            device_id=(other // naz, lax.rem(other, naz)), device_id_type=MESH,
        ).start()
        return carry

    lax.fori_loop(1, n, mail_out, 0)
    inbox[0] = post[me]

    loads[1].wait()
    pack_y(even, 0, 0)
    y_copy(0, 0).start()
    pack_y(even, 0, 1)
    y_copy(0, 1).start()

    def first_x(b, carry):
        pack_x(even, 0, b)
        send_x(0, b)
        return carry

    lax.fori_loop(0, 5, first_x, 0)
    loads[2].wait()

    def z_pass(cur, nxt):
        def body(a, carry):
            for b in range(5):
                x = [[cur[f, a, b, r] for r in range(5)] for f in range(5)]
                dw = deriv(x[3])
                dg = deriv([MACH * x[1][r] + x[0][r] for r in range(5)])
                lo = cross_terms(
                    [x[f][0] - jnp.where(lane == 0, 0.0, pltpu.roll(x[f][4], 1, 1)) for f in range(5)],
                    -1.0, 3,
                )
                hi = cross_terms(
                    [x[f][4] - jnp.where(lane == 127, 0.0, pltpu.roll(x[f][0], 127, 1)) for f in range(5)],
                    1.0, 3,
                )
                for r in range(5):
                    for f in range(5):
                        value = dw[r] if f in (0, 4) else dg[r] if f == 3 else None
                        face = lo[f] if r == 0 else hi[f] if r == 4 else None
                        if value is None:
                            value = jnp.zeros((8, 128), F32) if face is None else face
                        elif face is not None:
                            value = value + face
                        nxt[f, a, b, r] = value
            return carry

        lax.fori_loop(0, 5, body, 0)

    def y_pass(cur, nxt):
        def body(a, carry):
            for r in range(5):
                x = [[cur[f, a, b, r] for b in range(5)] for f in range(5)]
                dv = deriv(x[2])
                dg = deriv([MACH * x[1][b] + x[0][b] for b in range(5)])
                jump_lo, jump_hi = [], []
                for f in range(5):
                    jump_lo.append(x[f][0] - jnp.where(ey == 0, 0.0, pltpu.roll(x[f][4], 1, 0)))
                    jump_hi.append(x[f][4] - jnp.where(ey == 3, 0.0, pltpu.roll(x[f][0], 7, 0)))
                lo, hi = cross_terms(jump_lo, -1.0, 2), cross_terms(jump_hi, 1.0, 2)
                ready = []
                for b in range(5):
                    for f in range(5):
                        value = dv[b] if f in (0, 4) else dg[b] if f == 2 else None
                        face = lo[f] if b == 0 else hi[f] if b == 4 else None
                        if value is None and face is None:
                            continue
                        if value is None:
                            value = face
                        elif face is not None:
                            value = value + face
                        ready.append((f, b, nxt[f, a, b, r] + value))
                for f, b, value in ready:
                    nxt[f, a, b, r] = value
            return carry

        lax.fori_loop(0, 5, body, 0)

    def y_fix(nxt, k, side):
        b, normal, edge = (0, -1.0, 0) if side == 0 else (4, 1.0, 3)
        y_copy(k, side).wait_recv()

        def body(a, carry):
            faces = unpack_faces(yl if side == 0 else yr, (k, a), 4)
            for r in range(5):
                jump = []
                for f in range(5):
                    q = 5 * r + f
                    j = q % 4
                    halo = pltpu.roll(faces[q // 4], 8 - j, 0) if j else faces[q // 4]
                    jump.append(jnp.where(ey == edge, -halo, 0.0))
                ready = [nxt[f, a, b, r] + t for f, t in enumerate(cross_terms(jump, normal, 2))]
                for f in range(5):
                    nxt[f, a, b, r] = ready[f]
            return carry

        lax.fori_loop(0, 5, body, 0)

    def x_pass(cur, nxt, k, scale):
        def body(i, carry):
            b = jnp.where(i == 3, 0, jnp.where(i == 4, 4, i + 1))

            @pl.when(i == 3)
            def _():
                y_fix(nxt, k, 0)

            @pl.when(i == 4)
            def _():
                y_fix(nxt, k, 1)

            take_x(k, b)
            left, right = unpack_faces(xl, (k, b), 7), unpack_faces(xr, (k, b), 7)
            for r in range(5):
                def emit(f, a, total):
                    if k == 0 and f in (1, 2, 3):
                        at = ((f - 1) * 125 + a * 25 + b * 5 + r) * 8
                        total = total + s_ref[pl.ds(pl.multiple_of(at, 8), 8), :]
                    total = scale * total
                    nxt[f, a, b, r] = total
                    acc[f, a, b, r] = acc[f, a, b, r] + total

                axial_lines(cur, nxt, left, right, b, r, low_half, emit)

            pack_x(nxt, k + 1, b)
            send_x(k + 1, b)

            @pl.when(i == 3)
            def _():
                pack_y(nxt, k + 1, 1)
                y_copy(k + 1, 1).start()

            @pl.when(i == 4)
            def _():
                pack_y(nxt, k + 1, 0)
                y_copy(k + 1, 0).start()
            return carry

        lax.fori_loop(0, 5, body, 0)

    def mail_block(first_one, many, g):
        return pltpu.make_async_remote_copy(
            src_ref=post.at[pl.ds(first_one, many), pl.ds(0, MAIL)],
            dst_ref=inbox.at[pl.ds(first_one, many), pl.ds(0, MAIL)],
            send_sem=mail_send, recv_sem=mail_recv.at[g],
            device_id=(ax, az), device_id_type=MESH,
        )

    def opened(g):
        block = inbox[pl.ds(g * GROUP, GROUP)]
        upper, lower = block[:, 0:8], block[:, 8:16]
        at = lax.broadcasted_iota(jnp.int32, (GROUP, 8, 128), 1)
        second = (upper << 16) >> 16
        first = (upper - second) >> 16
        third = jnp.where(at >= 6, upper, lower)
        early, late = pltpu.roll(third, 2, 1), pltpu.roll(third, 5, 1)
        third = jnp.where(at < 3, (early - ((early << 16) >> 16)) >> 16, (late << 16) >> 16)
        rows = [
            jnp.where(at < 6, x, 0).astype(F32).reshape(GROUP * 8, 128)
            for x in (first, second, third)
        ]
        code = rows[0][:, 125:126].astype(jnp.int32) - 1
        scale = jnp.exp2(-rows[1][:, 125:126])
        turned = jnp.concatenate([(x * scale).T for x in rows], axis=0)
        high = turned.astype(BF16)
        low = (turned - high.astype(F32)).astype(BF16)
        return code, jnp.concatenate([high, low], axis=1)

    def sums(code, lines, t):
        member = code == lax.broadcasted_iota(jnp.int32, (GROUP * 8, 256), 1) + 256 * t
        member = jnp.where(member, 1.0, 0.0).astype(BF16)
        return jnp.dot(
            lines, jnp.concatenate([member, member], axis=0), preferred_element_type=F32
        )

    def gather_first():
        mail_block(1, GROUP - 1, 0).wait_recv()
        code, lines = opened(0)
        for t in range(4):
            s_acc[:, 256 * t:256 * t + 256] = sums(code, lines, t)

    def gather(g, carry):
        mail_block(g * GROUP, GROUP, g).wait_recv()
        code, lines = opened(g)
        for t in range(4):
            s_acc[:, 256 * t:256 * t + 256] += sums(code, lines, t)
        return carry

    def gather_last():
        mail_block((groups - 1) * GROUP, GROUP, groups - 1).wait_recv()
        code, lines = opened(groups - 1)
        for t in range(4):
            total = s_acc[:, 256 * t:256 * t + 256] + sums(code, lines, t)
            for c in range(3):
                for h in range(2):
                    s_ref[pl.ds(c * 1000 + 2 * t + h, 125, stride=8), :] = total[
                        128 * c:128 * c + 125, 128 * h:128 * h + 128
                    ]

    for k in range(4):
        cur, nxt = (even, odd) if k % 2 == 0 else (odd, even)
        z_pass(cur, nxt)
        y_pass(cur, nxt)
        if k == 0:
            gather_first()
            lax.fori_loop(1, groups - 1, gather, 0)
            gather_last()
        if k < 3:
            x_pass(cur, nxt, k, DT / (k + 1))

    mail_block(0, n - 1, 0).wait_send()

    def drain(k, carry):
        y_copy(k, 0).wait_send()
        y_copy(k, 1).wait_send()

        def inner(b, carry):
            @pl.when(has_right)
            def _():
                x_copy(k, b, 0).wait_send()

            @pl.when(has_left)
            def _():
                x_copy(k, b, 1).wait_send()
            return carry

        lax.fori_loop(0, 5, inner, 0)
        return carry

    lax.fori_loop(0, 4, drain, 0)
    y_fix(even, 3, 0)
    y_fix(even, 3, 1)
    for b in range(5):
        take_x(3, b)


def finish(nxt, cur, acc, s_ref, xl, xr, new_hbm, source_hbm, new_ref, sem):
    save_source = pltpu.make_async_copy(s_ref, source_hbm, sem.at[5])
    save_source.start()
    low_half = lax.broadcasted_iota(jnp.int32, (8, 128), 0) < 4

    def save(b):
        return pltpu.make_async_copy(new_ref.at[:, :, b], new_hbm.at[:, :, b], sem.at[b])

    def body(b, carry):
        left, right = unpack_faces(xl, (3, b), 7), unpack_faces(xr, (3, b), 7)
        for r in range(5):
            def emit(f, a, total):
                new_ref[f, a, b, r] = acc[f, a, b, r] + (DT / 4.0) * total

            axial_lines(cur, nxt, left, right, b, r, low_half, emit)
        save(b).start()
        return carry

    lax.fori_loop(0, 5, body, 0)
    for b in range(5):
        save(b).wait()
    save_source.wait()


def body(nax, naz, lamb_vector, owner, element, shape_class, interp_tables, acoustic_state):
    n = nax * naz
    count = lamb_vector.shape[0]
    lamb = jnp.transpose(lamb_vector, (1, 0, 2))
    table = jnp.pad(jnp.transpose(interp_tables, (0, 2, 1)), ((0, 0), (0, 3), (0, 0)))
    table = table.reshape(256, 512)
    nodes = (5, 5, 5, 5, 8, 128)
    state = acoustic_state.reshape(nodes)
    key = ((element * 2 + shape_class) * n + owner[:, 0]).reshape(1, count)
    vmem, hbm = pl.BlockSpec(memory_space=pltpu.VMEM), pl.BlockSpec(memory_space=pltpu.HBM)
    dma = pltpu.SemaphoreType.DMA
    kept = pl.pallas_call(
        functools.partial(kernel, nax, naz),
        out_shape=(
            jax.ShapeDtypeStruct(nodes, F32),
            jax.ShapeDtypeStruct(nodes, F32),
            jax.ShapeDtypeStruct(nodes, F32),
            jax.ShapeDtypeStruct((3000, 128), F32),
            jax.ShapeDtypeStruct((4, 5, 112, 128), BF16),
            jax.ShapeDtypeStruct((4, 5, 112, 128), BF16),
        ),
        in_specs=[hbm, hbm, vmem, vmem],
        out_specs=(vmem,) * 6,
        scratch_shapes=[
            pltpu.VMEM(lamb.shape, BF16),
            pltpu.VMEM((384, 1024), F32),
            pltpu.VMEM((n, 16, 128), jnp.int32),
            pltpu.VMEM((n, 16, 128), jnp.int32),
            pltpu.VMEM((4, 5, 2, 112, 128), BF16),
            pltpu.VMEM((4, 2, 5, 64, 128), BF16),
            pltpu.VMEM((4, 5, 64, 128), BF16),
            pltpu.VMEM((4, 5, 64, 128), BF16),
            dma((3,)), dma, dma((n // GROUP,)),
            dma((4, 5, 2)), dma((4, 5, 2)), dma((4, 2)), dma((4, 2)),
        ],
        compiler_params=pltpu.CompilerParams(
            collective_id=0, has_side_effects=True, vmem_limit_bytes=36 * 1024 * 1024
        ),
    )(state, lamb, key, table)
    new, source = pl.pallas_call(
        finish,
        out_shape=(jax.ShapeDtypeStruct(nodes, F32), jax.ShapeDtypeStruct((3000, 128), F32)),
        in_specs=[vmem] * 6,
        out_specs=(hbm, hbm),
        scratch_shapes=[pltpu.VMEM(nodes, F32), dma((6,))],
        compiler_params=pltpu.CompilerParams(vmem_limit_bytes=24 * 1024 * 1024),
    )(*kept)
    return new.reshape(5, 125, 2, 4, 128), source.reshape(3, 125, 2, 4, 128)


def solution(mesh):
    nax, naz = mesh.shape["ax"], mesh.shape["az"]
    in_specs = (
        P(("ax", "az"), None, None),
        P(("ax", "az"), None),
        P(("ax", "az")),
        P(("ax", "az")),
        P(),
        P(None, None, "ax", "az", None),
    )
    out_specs = (P(None, None, "ax", "az", None), P(None, None, "ax", "az", None))
    return jax.shard_map(
        functools.partial(body, nax, naz), mesh=mesh, in_specs=in_specs, out_specs=out_specs,
        check_vma=False,
    )
```

```python
import functools
import math

import jax
import jax.numpy as jnp
import numpy as np
from jax import lax
from jax.experimental import pallas as pl
from jax.experimental.pallas import tpu as pltpu
from jax.sharding import PartitionSpec as P

MACH = 0.3
SPEED = 1.3
DT = 0.03
LIFT = 10.0
VOLUME = 2.0
MAIL = 9
GROUP = 32
MESH = pl.DeviceIdType.MESH
F32 = jnp.float32
BF16 = jnp.bfloat16


def line_matrix():
    points = [-1.0, -math.sqrt(3.0 / 7.0), 0.0, math.sqrt(3.0 / 7.0), 1.0]
    bary = [
        1.0 / math.prod(points[c] - points[o] for o in range(5) if o != c) for c in range(5)
    ]
    d = np.zeros((5, 5))
    for i in range(5):
        for j in range(5):
            if i != j:
                d[i, j] = bary[j] / bary[i] / (points[i] - points[j])
        d[i, i] = -np.sum(d[i])
    return -VOLUME * d


D = line_matrix()


def deriv(x):
    e0, e1, o0, o1 = x[0] + x[4], x[1] + x[3], x[0] - x[4], x[1] - x[3]
    y = [None] * 5
    for i in range(2):
        odd = float(0.5 * (D[i, 0] - D[i, 4])) * o0 + float(0.5 * (D[i, 1] - D[i, 3])) * o1
        even = (
            float(0.5 * (D[i, 0] + D[i, 4])) * e0
            + float(0.5 * (D[i, 1] + D[i, 3])) * e1
            + float(D[i, 2]) * x[2]
        )
        y[i], y[4 - i] = odd + even, odd - even
    y[2] = float(D[2, 0]) * o0 + float(D[2, 1]) * o1
    return y


def cross_terms(jump, normal, along):
    t = (LIFT * normal) * jump[along]
    out = [None] * 5
    for f in (0, 4):
        out[f] = t - (LIFT * SPEED) * jump[f]
    for f in (1, 2, 3):
        out[f] = (-LIFT * SPEED) * jump[f]
    g = MACH * jump[1] + jump[0]
    out[along] = out[along] + (LIFT * normal) * g
    return out


def axial_terms(jump, normal):
    p, u, v, w, d = jump
    near = LIFT * (normal * MACH - SPEED)
    t = (LIFT * normal) * u
    return [
        near * p + t,
        near * u + (LIFT * normal) * p,
        (-LIFT * SPEED) * v,
        (-LIFT * SPEED) * w,
        near * d + t,
    ]


def unpack_faces(ref, index, tiles):
    parts = []
    for t in range(tiles):
        wide = ref[index + (slice(16 * t, 16 * t + 16), slice(None))].astype(F32)
        parts += [wide[:8], wide[8:]]
    return parts


def axial_lines(cur, nxt, left, right, b, r, low_half, emit):
    x = [[cur[f, a, b, r] for a in range(5)] for f in range(5)]
    p, u, d = x[0], x[1], x[4]
    diff = {
        0: deriv([MACH * p[a] + u[a] for a in range(5)]),
        1: deriv([MACH * u[a] + p[a] for a in range(5)]),
        4: deriv([MACH * d[a] + u[a] for a in range(5)]),
    }
    jump_lo, jump_hi = [], []
    for f in range(5):
        q = 5 * r + f
        m = q // 2
        if q % 2 == 0:
            halo = jnp.where(low_half, left[m], right[m])
        else:
            halo = pltpu.roll(jnp.where(low_half, right[m], left[m]), 4, 0)
        own = pltpu.roll(jnp.where(low_half, x[f][4], x[f][0]), 4, 0)
        jump_lo.append(x[f][0] - jnp.where(low_half, halo, own))
        jump_hi.append(x[f][4] - jnp.where(low_half, own, halo))
    lo, hi = axial_terms(jump_lo, -1.0), axial_terms(jump_hi, 1.0)
    for a in range(5):
        for f in range(5):
            total = nxt[f, a, b, r]
            if f in diff:
                total = total + diff[f][a]
            if a in (0, 4):
                total = total + (lo[f] if a == 0 else hi[f])
            emit(f, a, total)


def kernel(
    nax, naz,
    state_hbm, lamb_hbm, key_ref, table_ref,
    even, odd, acc, s_ref, xl, xr,
    lamb_ref, s_acc, post, inbox,
    xs, ys, yl, yr,
    load_sem, mail_send, mail_recv, xsend, xrecv, ysend, yrecv,
):
    n = nax * naz
    groups = n // GROUP
    ax, az = lax.axis_index("ax"), lax.axis_index("az")
    me = ax * naz + az
    has_left, has_right = ax > 0, ax < nax - 1
    az_up, az_down = lax.rem(az + 1, naz), lax.rem(az + naz - 1, naz)
    row = lax.broadcasted_iota(jnp.int32, (8, 128), 0)
    lane = lax.broadcasted_iota(jnp.int32, (8, 128), 1)
    low_half = row < 4
    ey = row & 3

    loads = [
        pltpu.make_async_copy(src, dst, load_sem.at[i])
        for i, (src, dst) in enumerate(
            [(lamb_hbm, lamb_ref), (state_hbm, even), (state_hbm, acc)]
        )
    ]
    for load in loads:
        load.start()

    barrier = pltpu.get_barrier_semaphore()

    def greet(i, carry):
        other = lax.rem(me + i, n)
        pl.semaphore_signal(
            barrier, inc=1, device_id=(other // naz, lax.rem(other, naz)), device_id_type=MESH
        )
        return carry

    lax.fori_loop(1, n, greet, 0)

    @pl.when(jnp.logical_not(has_left))
    def _():
        def body(i, carry):
            for k in range(4):
                xl[k, i] = jnp.zeros(xl.shape[2:], BF16)
            return carry
        lax.fori_loop(0, 5, body, 0)

    @pl.when(jnp.logical_not(has_right))
    def _():
        def body(i, carry):
            for k in range(4):
                xr[k, i] = jnp.zeros(xr.shape[2:], BF16)
            return carry
        lax.fori_loop(0, 5, body, 0)

    key = key_ref[...]
    owner, element, shape_class = lax.rem(key, n), (key // n) >> 1, (key // n) & 1
    count = owner.shape[1]
    hit = lax.broadcasted_iota(jnp.int32, (n, count), 0) == owner
    hit = jnp.where(hit, 1.0, 0.0)
    earlier = lax.broadcasted_iota(jnp.int32, (count, count), 0) < lax.broadcasted_iota(
        jnp.int32, (count, count), 1
    )
    ranks = jnp.dot(
        hit.astype(BF16), jnp.where(earlier, 1.0, 0.0).astype(BF16), preferred_element_type=F32
    )
    position = jnp.sum(hit * ranks, axis=0, keepdims=True).astype(jnp.int32)
    values, largest = [], None
    loads[0].wait()
    for c in range(3):
        both = lax.dot_general(
            table_ref[...], lamb_ref[c], (((1,), (1,)), ((), ())), preferred_element_type=F32
        )
        value = jnp.where(shape_class == 0, both[:128], both[128:])
        values.append(value)
        top = jnp.max(jnp.abs(value), axis=0, keepdims=True)
        largest = top if largest is None else jnp.maximum(largest, top)
    shift = 14.0 - jnp.floor(jnp.log2(jnp.maximum(largest, 1e-30)))
    gain = jnp.exp2(shift)
    node_row = lax.broadcasted_iota(jnp.int32, (128, count), 0)
    digits = []
    for c in range(3):
        fixed = jnp.clip(jnp.floor(values[c] * gain + 0.5), -32767.0, 32767.0)
        if c == 0:
            fixed = jnp.where(node_row == 125, (element + 1).astype(F32), fixed)
        if c == 1:
            fixed = jnp.where(node_row == 125, shift, fixed)
        high = jnp.floor((fixed + 128.0) * (1.0 / 256.0))
        digits.append([high.astype(BF16), (fixed - 256.0 * high).astype(BF16)])
    slot_row = lax.broadcasted_iota(jnp.int32, (n * 8, count), 0)

    def placed(slot, fields):
        place = jnp.where(slot_row == slot, 1.0, 0.0).astype(BF16)
        out = []
        for c in fields:
            mail = lax.dot_general(
                place, jnp.concatenate(digits[c], axis=0), (((1,), (1,)), ((), ())),
                preferred_element_type=F32,
            )
            out.append((256.0 * mail[:, :128] + mail[:, 128:]).astype(jnp.int32))
        return out

    early = position < 3
    first, second = placed(owner * 8 + position, (0, 1))
    (upper,) = placed(jnp.where(early, owner * 8 + ((position + 6) & 7), -1), (2,))
    (lower,) = placed(jnp.where(early, -1, owner * 8 + ((position + 3) & 7)), (2,))
    pair = ((first << 16) + second).reshape(n, 8, 128)
    third = ((upper << 16) + lower).reshape(n, 8, 128)
    tile_row = lax.broadcasted_iota(jnp.int32, (n, 8, 128), 1)
    post[:, 0:8] = jnp.where(tile_row < 6, pair, third)
    post[:, 8:16] = third

    def x_copy(k, b, side):
        if side == 0:
            dst, dev = xl, (ax + 1, az)
        else:
            dst, dev = xr, (ax - 1, az)
        return pltpu.make_async_remote_copy(
            src_ref=xs.at[k, b, side], dst_ref=dst.at[k, b], send_sem=xsend.at[k, b, side],
            recv_sem=xrecv.at[k, b, side], device_id=dev, device_id_type=MESH,
        )

    def y_copy(k, side):
        if side == 0:
            dst, dev = yl, (ax, az_up)
        else:
            dst, dev = yr, (ax, az_down)
        return pltpu.make_async_remote_copy(
            src_ref=ys.at[k, side], dst_ref=dst.at[k], send_sem=ysend.at[k, side],
            recv_sem=yrecv.at[k, side], device_id=dev, device_id_type=MESH,
        )

    def pack_x(ref, k, b):
        for side in range(2):
            a = 4 if side == 0 else 0
            parts = []
            for m in range(14):
                pair = []
                for q in (2 * m, 2 * m + 1):
                    pair.append(ref[q % 5, a, b, q // 5] if q < 25 else jnp.zeros((8, 128), F32))
                even, odd = pltpu.roll(pair[0], 4, 0), pair[1]
                parts.append(
                    jnp.where(low_half, even, odd) if side == 0 else jnp.where(low_half, odd, even)
                )
            for t in range(7):
                xs[k, b, side, 16 * t:16 * t + 16, :] = jnp.concatenate(
                    [parts[2 * t], parts[2 * t + 1]], axis=0
                ).astype(BF16)

    def pack_y(ref, k, side):
        b = 4 if side == 0 else 0

        def body(a, carry):
            parts = []
            for m in range(8):
                total = jnp.zeros((8, 128), F32)
                for j in range(4):
                    q = 4 * m + j
                    if q < 25:
                        turn = (j - 3) % 8 if side == 0 else (3 + j) % 8
                        value = ref[q % 5, a, b, q // 5]
                        value = pltpu.roll(value, turn, 0) if turn else value
                        residue = j if side == 0 else (3 + j) % 4
                        total = jnp.where(ey == residue, value, total)
                parts.append(total)
            for t in range(4):
                ys[k, side, a, 16 * t:16 * t + 16, :] = jnp.concatenate(
                    [parts[2 * t], parts[2 * t + 1]], axis=0
                ).astype(BF16)
            return carry

        lax.fori_loop(0, 5, body, 0)

    def send_x(k, b):
        @pl.when(has_right)
        def _():
            x_copy(k, b, 0).start()

        @pl.when(has_left)
        def _():
            x_copy(k, b, 1).start()

    def take_x(k, b):
        @pl.when(has_left)
        def _():
            x_copy(k, b, 0).wait_recv()

        @pl.when(has_right)
        def _():
            x_copy(k, b, 1).wait_recv()

    pl.semaphore_wait(barrier, n - 1)

    def mail_out(i, carry):
        other = lax.rem(me + 37 * i, n)
        pltpu.make_async_remote_copy(
            src_ref=post.at[other, pl.ds(0, MAIL)], dst_ref=inbox.at[i, pl.ds(0, MAIL)],
            send_sem=mail_send, recv_sem=mail_recv.at[i // GROUP],
            device_id=(other // naz, lax.rem(other, naz)), device_id_type=MESH,
        ).start()
        return carry

    lax.fori_loop(1, n, mail_out, 0)
    inbox[0] = post[me]

    loads[1].wait()
    pack_y(even, 0, 0)
    y_copy(0, 0).start()
    pack_y(even, 0, 1)
    y_copy(0, 1).start()

    def first_x(b, carry):
        pack_x(even, 0, b)
        send_x(0, b)
        return carry

    lax.fori_loop(0, 5, first_x, 0)
    loads[2].wait()

    def z_pass(cur, nxt):
        def body(a, carry):
            for b in range(5):
                x = [[cur[f, a, b, r] for r in range(5)] for f in range(5)]
                dw = deriv(x[3])
                dg = deriv([MACH * x[1][r] + x[0][r] for r in range(5)])
                lo = cross_terms(
                    [x[f][0] - jnp.where(lane == 0, 0.0, pltpu.roll(x[f][4], 1, 1)) for f in range(5)],
                    -1.0, 3,
                )
                hi = cross_terms(
                    [x[f][4] - jnp.where(lane == 127, 0.0, pltpu.roll(x[f][0], 127, 1)) for f in range(5)],
                    1.0, 3,
                )
                for r in range(5):
                    for f in range(5):
                        value = dw[r] if f in (0, 4) else dg[r] if f == 3 else None
                        face = lo[f] if r == 0 else hi[f] if r == 4 else None
                        if value is None:
                            value = jnp.zeros((8, 128), F32) if face is None else face
                        elif face is not None:
                            value = value + face
                        nxt[f, a, b, r] = value
            return carry

        lax.fori_loop(0, 5, body, 0)

    def y_pass(cur, nxt):
        def body(a, carry):
            for r in range(5):
                x = [[cur[f, a, b, r] for b in range(5)] for f in range(5)]
                dv = deriv(x[2])
                dg = deriv([MACH * x[1][b] + x[0][b] for b in range(5)])
                jump_lo, jump_hi = [], []
                for f in range(5):
                    jump_lo.append(x[f][0] - jnp.where(ey == 0, 0.0, pltpu.roll(x[f][4], 1, 0)))
                    jump_hi.append(x[f][4] - jnp.where(ey == 3, 0.0, pltpu.roll(x[f][0], 7, 0)))
                lo, hi = cross_terms(jump_lo, -1.0, 2), cross_terms(jump_hi, 1.0, 2)
                ready = []
                for b in range(5):
                    for f in range(5):
                        value = dv[b] if f in (0, 4) else dg[b] if f == 2 else None
                        face = lo[f] if b == 0 else hi[f] if b == 4 else None
                        if value is None and face is None:
                            continue
                        if value is None:
                            value = face
                        elif face is not None:
                            value = value + face
                        ready.append((f, b, nxt[f, a, b, r] + value))
                for f, b, value in ready:
                    nxt[f, a, b, r] = value
            return carry

        lax.fori_loop(0, 5, body, 0)

    def y_fix(nxt, k, side):
        b, normal, edge = (0, -1.0, 0) if side == 0 else (4, 1.0, 3)
        y_copy(k, side).wait_recv()

        def body(a, carry):
            faces = unpack_faces(yl if side == 0 else yr, (k, a), 4)
            for r in range(5):
                jump = []
                for f in range(5):
                    q = 5 * r + f
                    j = q % 4
                    halo = pltpu.roll(faces[q // 4], 8 - j, 0) if j else faces[q // 4]
                    jump.append(jnp.where(ey == edge, -halo, 0.0))
                ready = [nxt[f, a, b, r] + t for f, t in enumerate(cross_terms(jump, normal, 2))]
                for f in range(5):
                    nxt[f, a, b, r] = ready[f]
            return carry

        lax.fori_loop(0, 5, body, 0)

    def x_pass(cur, nxt, k, scale):
        def body(i, carry):
            b = jnp.where(i == 3, 0, jnp.where(i == 4, 4, i + 1))

            @pl.when(i == 3)
            def _():
                y_fix(nxt, k, 0)

            @pl.when(i == 4)
            def _():
                y_fix(nxt, k, 1)

            take_x(k, b)
            left, right = unpack_faces(xl, (k, b), 7), unpack_faces(xr, (k, b), 7)
            for r in range(5):
                def emit(f, a, total):
                    if k == 0 and f in (1, 2, 3):
                        at = ((f - 1) * 125 + a * 25 + b * 5 + r) * 8
                        total = total + s_ref[pl.ds(pl.multiple_of(at, 8), 8), :]
                    total = scale * total
                    nxt[f, a, b, r] = total
                    acc[f, a, b, r] = acc[f, a, b, r] + total

                axial_lines(cur, nxt, left, right, b, r, low_half, emit)

            pack_x(nxt, k + 1, b)
            send_x(k + 1, b)

            @pl.when(i == 3)
            def _():
                pack_y(nxt, k + 1, 1)
                y_copy(k + 1, 1).start()

            @pl.when(i == 4)
            def _():
                pack_y(nxt, k + 1, 0)
                y_copy(k + 1, 0).start()
            return carry

        lax.fori_loop(0, 5, body, 0)

    def mail_block(first_one, many, g):
        return pltpu.make_async_remote_copy(
            src_ref=post.at[pl.ds(first_one, many), pl.ds(0, MAIL)],
            dst_ref=inbox.at[pl.ds(first_one, many), pl.ds(0, MAIL)],
            send_sem=mail_send, recv_sem=mail_recv.at[g],
            device_id=(ax, az), device_id_type=MESH,
        )

    def opened(g):
        block = inbox[pl.ds(g * GROUP, GROUP)]
        upper, lower = block[:, 0:8], block[:, 8:16]
        at = lax.broadcasted_iota(jnp.int32, (GROUP, 8, 128), 1)
        second = (upper << 16) >> 16
        first = (upper - second) >> 16
        third = jnp.where(at >= 6, upper, lower)
        early, late = pltpu.roll(third, 2, 1), pltpu.roll(third, 5, 1)
        third = jnp.where(at < 3, (early - ((early << 16) >> 16)) >> 16, (late << 16) >> 16)
        rows = [
            jnp.where(at < 6, x, 0).astype(F32).reshape(GROUP * 8, 128)
            for x in (first, second, third)
        ]
        code = rows[0][:, 125:126].astype(jnp.int32) - 1
        scale = jnp.exp2(-rows[1][:, 125:126])
        turned = jnp.concatenate([(x * scale).T for x in rows], axis=0)
        high = turned.astype(BF16)
        low = (turned - high.astype(F32)).astype(BF16)
        return code, jnp.concatenate([high, low], axis=1)

    def sums(code, lines, t):
        member = code == lax.broadcasted_iota(jnp.int32, (GROUP * 8, 256), 1) + 256 * t
        member = jnp.where(member, 1.0, 0.0).astype(BF16)
        return jnp.dot(
            lines, jnp.concatenate([member, member], axis=0), preferred_element_type=F32
        )

    def gather_first():
        mail_block(1, GROUP - 1, 0).wait_recv()
        code, lines = opened(0)
        for t in range(4):
            s_acc[:, 256 * t:256 * t + 256] = sums(code, lines, t)

    def gather(g, carry):
        mail_block(g * GROUP, GROUP, g).wait_recv()
        code, lines = opened(g)
        for t in range(4):
            s_acc[:, 256 * t:256 * t + 256] += sums(code, lines, t)
        return carry

    def gather_last():
        mail_block((groups - 1) * GROUP, GROUP, groups - 1).wait_recv()
        code, lines = opened(groups - 1)
        for t in range(4):
            total = s_acc[:, 256 * t:256 * t + 256] + sums(code, lines, t)
            for c in range(3):
                for h in range(2):
                    s_ref[pl.ds(c * 1000 + 2 * t + h, 125, stride=8), :] = total[
                        128 * c:128 * c + 125, 128 * h:128 * h + 128
                    ]

    for k in range(4):
        cur, nxt = (even, odd) if k % 2 == 0 else (odd, even)
        z_pass(cur, nxt)
        y_pass(cur, nxt)
        if k == 0:
            gather_first()
            lax.fori_loop(1, groups - 1, gather, 0)
            gather_last()
        if k < 3:
            x_pass(cur, nxt, k, DT / (k + 1))

    mail_block(0, n - 1, 0).wait_send()

    def drain(k, carry):
        y_copy(k, 0).wait_send()
        y_copy(k, 1).wait_send()

        def inner(b, carry):
            @pl.when(has_right)
            def _():
                x_copy(k, b, 0).wait_send()

            @pl.when(has_left)
            def _():
                x_copy(k, b, 1).wait_send()
            return carry

        lax.fori_loop(0, 5, inner, 0)
        return carry

    lax.fori_loop(0, 4, drain, 0)
    y_fix(even, 3, 0)
    y_fix(even, 3, 1)
    for b in range(5):
        take_x(3, b)


def finish(nxt, cur, acc, s_ref, xl, xr, new_hbm, source_hbm, new_ref, sem):
    save_source = pltpu.make_async_copy(s_ref, source_hbm, sem.at[5])
    save_source.start()
    low_half = lax.broadcasted_iota(jnp.int32, (8, 128), 0) < 4

    def save(b):
        return pltpu.make_async_copy(new_ref.at[:, :, b], new_hbm.at[:, :, b], sem.at[b])

    def body(b, carry):
        left, right = unpack_faces(xl, (3, b), 7), unpack_faces(xr, (3, b), 7)
        for r in range(5):
            def emit(f, a, total):
                new_ref[f, a, b, r] = acc[f, a, b, r] + (DT / 4.0) * total

            axial_lines(cur, nxt, left, right, b, r, low_half, emit)
        save(b).start()
        return carry

    lax.fori_loop(0, 5, body, 0)
    for b in range(5):
        save(b).wait()
    save_source.wait()


def body(nax, naz, lamb_vector, owner, element, shape_class, interp_tables, acoustic_state):
    n = nax * naz
    count = lamb_vector.shape[0]
    lamb = jnp.transpose(lamb_vector, (1, 0, 2))
    table = jnp.pad(jnp.transpose(interp_tables, (0, 2, 1)), ((0, 0), (0, 3), (0, 0)))
    table = table.reshape(256, 512)
    nodes = (5, 5, 5, 5, 8, 128)
    state = acoustic_state.reshape(nodes)
    key = ((element * 2 + shape_class) * n + owner[:, 0]).reshape(1, count)
    vmem, hbm = pl.BlockSpec(memory_space=pltpu.VMEM), pl.BlockSpec(memory_space=pltpu.HBM)
    dma = pltpu.SemaphoreType.DMA
    kept = pl.pallas_call(
        functools.partial(kernel, nax, naz),
        out_shape=(
            jax.ShapeDtypeStruct(nodes, F32),
            jax.ShapeDtypeStruct(nodes, F32),
            jax.ShapeDtypeStruct(nodes, F32),
            jax.ShapeDtypeStruct((3000, 128), F32),
            jax.ShapeDtypeStruct((4, 5, 112, 128), BF16),
            jax.ShapeDtypeStruct((4, 5, 112, 128), BF16),
        ),
        in_specs=[hbm, hbm, vmem, vmem],
        out_specs=(vmem,) * 6,
        scratch_shapes=[
            pltpu.VMEM(lamb.shape, BF16),
            pltpu.VMEM((384, 1024), F32),
            pltpu.VMEM((n, 16, 128), jnp.int32),
            pltpu.VMEM((n, 16, 128), jnp.int32),
            pltpu.VMEM((4, 5, 2, 112, 128), BF16),
            pltpu.VMEM((4, 2, 5, 64, 128), BF16),
            pltpu.VMEM((4, 5, 64, 128), BF16),
            pltpu.VMEM((4, 5, 64, 128), BF16),
            dma((3,)), dma, dma((n // GROUP,)),
            dma((4, 5, 2)), dma((4, 5, 2)), dma((4, 2)), dma((4, 2)),
        ],
        compiler_params=pltpu.CompilerParams(
            collective_id=0, has_side_effects=True, vmem_limit_bytes=36 * 1024 * 1024
        ),
    )(state, lamb, key, table)
    new, source = pl.pallas_call(
        finish,
        out_shape=(jax.ShapeDtypeStruct(nodes, F32), jax.ShapeDtypeStruct((3000, 128), F32)),
        in_specs=[vmem] * 6,
        out_specs=(hbm, hbm),
        scratch_shapes=[pltpu.VMEM(nodes, F32), dma((6,))],
        compiler_params=pltpu.CompilerParams(vmem_limit_bytes=24 * 1024 * 1024),
    )(*kept)
    return new.reshape(5, 125, 2, 4, 128), source.reshape(3, 125, 2, 4, 128)


def solution(mesh):
    nax, naz = mesh.shape["ax"], mesh.shape["az"]
    in_specs = (
        P(("ax", "az"), None, None),
        P(("ax", "az"), None),
        P(("ax", "az")),
        P(("ax", "az")),
        P(),
        P(None, None, "ax", "az", None),
    )
    out_specs = (P(None, None, "ax", "az", None), P(None, None, "ax", "az", None))
    return jax.shard_map(
        functools.partial(body, nax, naz), mesh=mesh, in_specs=in_specs, out_specs=out_specs,
        check_vma=False,
    )
```
